512 devices in a mesh: user: 16 (over z, core), ctx: 8 (over y), head: 4 (over x).
Axes of the slice: x: 4, y: 8, z: 8, core: 2. Of those that a mesh axis runs over, the one named last changes fastest.
Arguments:
- catalog: bfloat16 [8192, 1024], P('user'), may hold values from -6 to 6
- cand_owner: int32 [16, 2048, 1], P('user', 'ctx'), may hold values from 0 to 15; in each aligned block of 256 rows (0 to 255, 256 to 511, ..., all dimensions but the last counted through in order) at most 32 rows name the same one
- cand_row: int32 [16, 2048], P('user', 'ctx'), may hold values from 0 to 511
- hist_len: int32 [16], P('user'), may hold values from 3072 to 12288, as said below
- proj_weight: bfloat16 [1024, 2, 1024], P(None, None, 'head'), may hold values from -0.1875 to 0.1875
- keys: bfloat16 [16, 12288, 1024], P('user', 'ctx', 'head'), may hold values from -6 to 6
- values: bfloat16 [16, 12288, 1024], P('user', 'ctx', 'head'), may hold values from -1280 to 1280
- out_weight: bfloat16 [1024, 1024], P('head'), may hold values from -0.1875 to 0.1875
Outputs:
- ranked: bfloat16 [16, 2048, 1024], P('user', 'ctx', 'head')
The draws below stay inside these ranges and needn't reach their ends.
Inputs may be any that keep to these rules, and one draw needn't show every extreme that they name: `cand_owner`: within each aligned block of 256 shortlisted items of one user (one ctx index), at most 32 are owned by the same catalog shard. `hist_len`: at least one user has all 12288 events.
All inputs are finite; a program needn't handle non-finite values.
Results may differ from the reference program's by a relative error of at most 0.0071.
Values may be sent and summed in bfloat16 or wider, within the bound.
A program may use at most 64 MiB of HBM per device.

```python
import math
import jax
import jax.numpy as jnp
import numpy as np
from jax import lax

D = 1024
HEAD = 128
CAND_DEV = 256
HIST_DEV = 1536
ROWS_DEV = 512
USERS = 16
CAND = 2048
HIST = 12288
ITEMS = 8192
CAP = 32
N_USER = 16
N_CTX = 8


def draw_hist_len(key, part):
    first_key, second_key = jax.random.split(jax.random.fold_in(key, 17))
    lengths = jax.random.randint(first_key, (USERS,), HIST // 4, HIST + 1)
    chosen = jax.random.randint(second_key, (), 0, USERS)
    return jnp.where(jnp.arange(USERS) == chosen, HIST, lengths).astype(jnp.int32)


def place_ends(array, key, smallest, top_value):
    longest = array.shape.index(max(array.shape))
    spots = []
    for shift in (0, 1):
        where = [jax.random.randint(jax.random.fold_in(key, axis), (), 0, length) for axis, length in enumerate(array.shape)]
        where[longest] = (where[longest] + shift) % array.shape[longest]
        spots.append(tuple(where))
    return array.at[spots[0]].set(smallest).at[spots[1]].set(top_value)


def steps_of(rng, extent, cuts, low, top_value):
    gain = 1.0
    for position, blocks in cuts:
        steps = jax.random.uniform(jax.random.fold_in(jax.random.fold_in(rng, 6), position), (blocks,), jnp.float32, low / len(cuts), top_value / len(cuts))
        gain = gain * jnp.repeat(jnp.exp(steps), extent[position] // blocks).reshape((-1,) + (1,) * (len(extent) - 1 - position))
    return gain


def assign_block(key, own, number, rows, amount, top, bound, skew):
    sequence = jax.random.permutation(key, amount)
    crowded, common = portions_of(amount, rows * top, bound, skew, True), portions_of(amount, rows * top, bound, skew, False)
    places = jnp.arange(amount)

    def named(tallies, offset_by):
        used = int((tallies > 0).sum())
        fixed = max(1, used // 4)
        moved = fixed + (places - fixed + offset_by * (used - fixed)) % max(1, amount - fixed)
        return jnp.zeros((amount,), jnp.int32).at[sequence[jnp.where(places < fixed, places, moved)]].set(jnp.asarray(tallies, jnp.int32))

    tallies = jnp.where(number % 4 == 0, named(crowded, number // 4), named(common, number - number // 4 - 1))
    mixed = jax.random.permutation(jax.random.fold_in(own, 3), amount)
    donor, sink = mixed[0:amount // 2 * 2:2], mixed[1:amount // 2 * 2:2]
    slack = jnp.minimum(tallies[donor] - 1, bound - tallies[sink]) // 2
    slack = jnp.where((donor == sequence[0]) | (sink == sequence[0]) | (tallies[sink] == 0), 0, jnp.maximum(slack, 0))
    moved = jax.random.randint(jax.random.fold_in(own, 4), (amount // 2,), 0, 1 << 20) % (slack + 1)
    tallies = tallies.at[donor].add(-moved).at[sink].add(moved)
    labels = jnp.searchsorted(jnp.cumsum(tallies), jnp.arange(rows * top), side="right").astype(jnp.int32)
    grid = labels.reshape(top, rows).T
    grid = grid[jax.random.permutation(jax.random.fold_in(own, 1), rows)]
    offset_by = jax.random.randint(jax.random.fold_in(own, 2), (rows, 1), 0, top)
    return jnp.take_along_axis(grid, (jnp.arange(top)[None, :] + offset_by) % top, axis=1)


def portions_of(amount, total, limit, slope, full):
    weights = [(1 << 20) // math.isqrt(grade ** slope) + 1 for grade in range(1, amount + 1)]
    largest = limit if full else min(limit, max(-(-total // amount), total * weights[0] // sum(weights)))
    least = 1 if total - largest >= amount - 1 else 0
    counts, rest = [largest] + [least] * (amount - 1), total - largest - least * (amount - 1)
    while rest > 0:
        movable = [i for i in range(1, amount) if counts[i] < largest] or [i for i in range(1, amount) if counts[i] < limit]
        mass, left = sum([weights[i] for i in movable]), rest
        for i in movable:
            extra = min(limit - counts[i], max(1, left * weights[i] // mass), rest)
            counts[i] = counts[i] + extra
            rest = rest - extra
    return np.array(counts)


def noise(stream_key, dims, deviation, limit, shards=(), kind=jnp.bfloat16):
    values = jax.random.normal(stream_key, dims, jnp.float32) * deviation
    if len(shards) > 0:
        values = steps_of(stream_key, dims, shards, -0.22, 0.18) * values
    return jnp.clip(values, min=-limit, max=limit).astype(kind)


def setup_inputs(seed: int = 0) -> dict:
    arg_keys = jax.random.split(jax.random.key(seed), 9)
    catalog = noise(arg_keys[0], (ITEMS, D), 1.0, 6.0, ((0, 16),))
    cand_owner_keys = jax.random.split(jax.random.fold_in(arg_keys[1], 1), USERS * CAND // CAND_DEV)
    cand_owner_turns = jax.random.permutation(jax.random.fold_in(arg_keys[1], 3), USERS * CAND // CAND_DEV)
    cand_owner = jax.vmap(lambda own, number: assign_block(jax.random.fold_in(arg_keys[1], 2), own, number, CAND_DEV, N_USER, 1, CAP, 1))(cand_owner_keys, cand_owner_turns).reshape((USERS, CAND, 1))
    cand_row = place_ends(jax.random.randint(arg_keys[2], (USERS, CAND), 0, ROWS_DEV), jax.random.fold_in(arg_keys[2], 1), 0, ROWS_DEV - 1).astype(jnp.int32)
    hist_len = draw_hist_len(jax.random.fold_in(arg_keys[8], 71), 0)
    proj_weight = noise(arg_keys[4], (D, 2, D), D ** -0.5, 0.1875, ((2, 4),))
    keys = noise(arg_keys[5], (USERS, HIST, D), 1.0, 6.0, ((0, 16), (1, 8), (2, 4)))
    values = noise(arg_keys[6], (USERS, HIST, D), (2 * (HIST_DEV * N_CTX) ** 0.5), 1280.0, ((0, 16), (1, 8), (2, 4)))
    out_weight = noise(arg_keys[7], (D, D), D ** -0.5, 0.1875, ((0, 4),))
    return {"catalog": catalog, "cand_owner": cand_owner, "cand_row": cand_row, "hist_len": hist_len, "proj_weight": proj_weight, "keys": keys, "values": values, "out_weight": out_weight}


def attend_user(query_rows, key_rows, value_rows, length):
    head_count = D // HEAD
    query_heads = query_rows.astype(jnp.float32).reshape(CAND, head_count, HEAD)
    length_float = length.astype(jnp.float32)

    def add_block(running, block_index):
        row_start = (block_index * HIST_DEV).astype(jnp.int32)
        key_block = lax.dynamic_slice_in_dim(key_rows, row_start, HIST_DEV, 0).astype(jnp.float32).reshape(HIST_DEV, head_count, HEAD)
        value_block = lax.dynamic_slice_in_dim(value_rows, row_start, HIST_DEV, 0).astype(jnp.float32).reshape(HIST_DEV, head_count, HEAD)
        scores = jnp.einsum("rhc,nhc->rhn", query_heads, key_block) * (HEAD ** -0.5)
        places = row_start + jnp.arange(HIST_DEV, dtype=jnp.int32)
        weights = jnp.where(places[None, None, :] < length, jax.nn.silu(scores) / length_float, 0.0).astype(jnp.bfloat16)
        weights = lax.optimization_barrier(weights).astype(jnp.float32)
        return running + jnp.einsum("rhn,nhc->rhc", weights, value_block), None

    running, unused = lax.scan(add_block, jnp.zeros((CAND, head_count, HEAD), jnp.float32), jnp.arange(N_CTX, dtype=jnp.int32))
    return running.reshape(CAND, D)


def reference(catalog, cand_owner, cand_row, hist_len, proj_weight, keys, values, out_weight):
    item_ids = (cand_owner[:, :, 0].astype(jnp.int32) * ROWS_DEV + cand_row.astype(jnp.int32)).reshape(-1)
    item_rows = jnp.take(catalog, item_ids, axis=0)
    pre_act = jnp.dot(item_rows, proj_weight.reshape(D, 2 * D), preferred_element_type=jnp.float32)
    projected = lax.optimization_barrier(jax.nn.silu(pre_act).astype(jnp.bfloat16)).reshape(USERS, CAND, 2, D)
    queries = projected[:, :, 0, :]
    gates = projected[:, :, 1, :]
    attended = lax.map(lambda packed: attend_user(packed[0], packed[1], packed[2], packed[3]), (queries, keys, values, hist_len))
    gated_rows = (attended * gates.astype(jnp.float32)).astype(jnp.bfloat16)
    ranked = jnp.dot(gated_rows.reshape(USERS * CAND, D), out_weight, preferred_element_type=jnp.float32)
    return ranked.astype(jnp.bfloat16).reshape(USERS, CAND, D)
```

```python
import functools

import jax
import jax.numpy as jnp
from jax import lax
from jax.experimental import pallas as pl
from jax.experimental.pallas import tpu as pltpu
from jax.sharding import PartitionSpec as P

HEAD = 128
MESH = pl.DeviceIdType.MESH
BF = jnp.bfloat16
F32 = jnp.float32
SLOTS = 32
KEY_STEP = 512


def send(src, dst, ssem, rsem, axis, index):
    return pltpu.make_async_remote_copy(
        src_ref=src, dst_ref=dst, send_sem=ssem, recv_sem=rsem,
        device_id={axis: index}, device_id_type=MESH,
    )


def column(row, lanes):
    tall = jnp.broadcast_to(row, (128, row.shape[1])).T
    return jnp.concatenate([tall] * (lanes // 128), axis=1)


def silu(v):
    return v / (1.0 + jnp.exp(-v))


def dot(a, b):
    return jnp.dot(a, b, preferred_element_type=F32)


def dot_t(a, b):
    return lax.dot_general(a, b, (((1,), (1,)), ((), ())), preferred_element_type=F32)


def kernel(
    n_user, n_ctx, n_head,
    cat_hbm, owner_ref, row_ref, len_ref, w_hbm, key_hbm, val_hbm, wout_hbm,
    out_ref,
    cat_v, w_v, key_v, val_v, wout_v,
    req_out, req_in, tab_q, tab_g, hot_v, unhot_v, sq, sg, rq, rg,
    q_all, acc, po, pin_l, pin_r, gate_v, g_all, wx,
    load_sem, req_ss, req_rs, sq_ss, sq_rs, sg_ss, sg_rs,
    ag_ss, ag_rs, rs_ss, rs_rs, wx_ss, wx_rs, xg_ss, xg_rs,
):
    u = lax.axis_index("user")
    c = lax.axis_index("ctx")
    h = lax.axis_index("head")
    right, left = lax.rem(c + 1, n_ctx), lax.rem(c + n_ctx - 1, n_ctx)
    cand = owner_ref.shape[1]
    half = cand // 2
    hist = key_v.shape[0]
    width = key_v.shape[1]
    slot_total = n_user * SLOTS

    loads = [
        pltpu.make_async_copy(a, b, load_sem.at[i])
        for i, (a, b) in enumerate(
            ((cat_hbm, cat_v), (w_hbm, w_v), (wout_hbm, wout_v), (key_hbm, key_v), (val_hbm, val_v))
        )
    ]
    for copy in loads:
        copy.start()

    barrier = pltpu.get_barrier_semaphore()

    def greet(d, _):
        pl.semaphore_signal(barrier, inc=1, device_id={"user": lax.rem(u + d, n_user)}, device_id_type=MESH)
        return 0

    lax.fori_loop(1, n_user, greet, 0)
    for other in (left, right):
        pl.semaphore_signal(barrier, inc=1, device_id={"ctx": other}, device_id_type=MESH)
    for k in range(1, n_head):
        pl.semaphore_signal(barrier, inc=1, device_id={"head": lax.rem(h + k, n_head)}, device_id_type=MESH)

    owner = owner_ref[...].astype(F32)
    owner_col = column(owner, cand)
    first = lax.broadcasted_iota(jnp.int32, (cand, cand), 0)
    second = lax.broadcasted_iota(jnp.int32, (cand, cand), 1)
    before = jnp.where((owner_col == owner) & (first < second), 1.0, 0.0)
    rank = jnp.sum(before, axis=0, keepdims=True)
    place_col = column(owner * SLOTS + rank, slot_total)
    slot_lane = lax.broadcasted_iota(jnp.int32, (cand, slot_total), 1).astype(F32)
    unhot_v[...] = jnp.where(place_col == slot_lane, 1.0, 0.0).astype(BF)
    rank_col = place_col[:, :128] - owner_col[:, :128] * SLOTS
    shift = (lax.rem(u, 4) * SLOTS).astype(F32)
    rank_hot = jnp.where(rank_col + shift == slot_lane[:, :128], 1.0, 0.0).astype(BF)
    wanted = row_ref[...]
    shard = lax.broadcasted_iota(jnp.int32, (n_user, cand), 0)
    mine = owner_ref[...] == shard
    high = jnp.where(mine, lax.shift_right_logical(wanted, 4).astype(F32), 0.0)
    low = jnp.where(mine, (wanted & 15).astype(F32), 0.0)
    asked = dot(jnp.concatenate([high, low], axis=0).astype(BF), rank_hot)
    asked = (asked[:n_user] * 16.0 + asked[n_user:]).astype(jnp.int32)
    for s in range(n_user):
        req_out[s] = asked[s:s + 1]

    pl.semaphore_wait(barrier, n_user - 1 + 2 + n_head - 1)

    def exchange(src, dst, ssem, rsem):
        def start(d, _):
            to = lax.rem(u + d, n_user)
            send(src.at[to], dst.at[u], ssem.at[d], rsem.at[d], "user", to).start()
            return 0

        lax.fori_loop(1, n_user, start, 0)
        dst[u] = src[u]

    def arrived(src, dst, ssem, rsem):
        def wait(d, _):
            origin = lax.rem(u + n_user - d, n_user)
            send(src.at[0], dst.at[origin], ssem.at[d], rsem.at[d], "user", lax.rem(u + d, n_user)).wait_recv()
            return 0

        lax.fori_loop(1, n_user, wait, 0)

    def drained(src, dst, ssem, rsem):
        def wait(d, _):
            to = lax.rem(u + d, n_user)
            send(src.at[to], dst.at[u], ssem.at[d], rsem.at[d], "user", to).wait_send()
            return 0

        lax.fori_loop(1, n_user, wait, 0)

    exchange(req_out, req_in, req_ss, req_rs)

    loads[0].wait()
    loads[1].wait()
    tab_q[...] = silu(dot(cat_v[...], w_v[0])).astype(BF)
    tab_g[...] = silu(dot(cat_v[...], w_v[1])).astype(BF)

    loads[2].wait()

    def wx_copy(k):
        to = lax.rem(h + k, n_head)
        cols = pl.ds(pl.multiple_of(to * width, width), width)
        return send(wout_v.at[:, cols], wx.at[k], wx_ss.at[k], wx_rs.at[k], "head", to)

    for k in range(1, n_head):
        wx_copy(k).start()
    wx[0] = wout_v[:, pl.ds(pl.multiple_of(h * width, width), width)]

    arrived(req_out, req_in, req_ss, req_rs)
    row_lane = lax.broadcasted_iota(jnp.int32, (128, cat_v.shape[0]), 1).astype(F32)
    for g in range(n_user // 4):
        ids = req_in[4 * g] + req_in[4 * g + 1] + req_in[4 * g + 2] + req_in[4 * g + 3]
        hot = jnp.where(column(ids.astype(F32), cat_v.shape[0]) == row_lane, 1.0, 0.0)
        hot_v[128 * g:128 * (g + 1)] = hot.astype(BF)
    sq[...] = dot(hot_v[...], tab_q[...]).astype(BF).reshape(sq.shape)
    exchange(sq, rq, sq_ss, sq_rs)
    sg[...] = dot(hot_v[...], tab_g[...]).astype(BF).reshape(sg.shape)
    exchange(sg, rg, sg_ss, sg_rs)

    loads[3].wait()
    loads[4].wait()
    length = len_ref[...]
    place = lax.broadcasted_iota(jnp.int32, (hist, width), 0) + c * hist
    val_v[...] = jnp.where(place < length, val_v[...].astype(F32), 0.0).astype(BF)
    scale = HEAD ** -0.5
    arg_scale = 0.5 * scale
    out_scale = jnp.broadcast_to((0.5 * scale) / length.astype(F32), (1, KEY_STEP))

    arrived(sq, rq, sq_ss, sq_rs)
    q_all[0] = dot(unhot_v[...], rq[...].reshape(slot_total, width)).astype(BF)

    def part(ref, block, ch):
        return ref.at[block, pl.ds(pl.multiple_of(ch * half, half), half)]

    def to_right(src_block, dst_block, ch, number):
        return send(part(q_all, src_block, ch), part(q_all, dst_block, ch),
                    ag_ss.at[0, number], ag_rs.at[0, number], "ctx", right)

    def to_left(src_block, dst_block, ch, number):
        return send(part(q_all, src_block, ch), part(q_all, dst_block, ch),
                    ag_ss.at[1, number], ag_rs.at[1, number], "ctx", left)

    for ch in (0, 1):
        to_right(0, 1, ch, ch + 1).start()
        to_left(0, n_ctx - 1, ch, ch + 1).start()

    def attend(block_a, ch_a, block_b, ch_b):
        queries = jnp.concatenate([part(q_all, block_a, ch_a)[...], part(q_all, block_b, ch_b)[...]], axis=0)
        totals = [None] * (width // HEAD)
        for k in range(hist // KEY_STEP):
            for n in range(width // HEAD):
                rows, cols = pl.ds(k * KEY_STEP, KEY_STEP), pl.ds(n * HEAD, HEAD)
                scores = dot_t(queries[:, n * HEAD:(n + 1) * HEAD], key_v[rows, cols])
                scaled = scores * out_scale
                weights = (scaled + scaled * jnp.tanh(scores * arg_scale)).astype(BF)
                term = dot(weights, val_v[rows, cols])
                totals[n] = term if totals[n] is None else totals[n] + term
        mixed = jnp.concatenate(totals, axis=1)
        part(acc, block_a, ch_a)[...] = mixed[:half]
        part(acc, block_b, ch_b)[...] = mixed[half:]

    attend(0, 0, 0, 1)

    def ring(t, _):
        k = lax.div(t + 1, 2)
        ch = lax.rem(t - 1, 2)
        to_right(0, k, ch, t).wait_recv()

        @pl.when(t <= 4)
        def _():
            to_right(k, k + 1, ch, t + 2).start()

        @pl.when(t == 5)
        def _():
            to_right(k, k + 1, ch, 7).start()

        to_left(0, n_ctx - k, ch, t).wait_recv()

        @pl.when(t <= 4)
        def _():
            to_left(n_ctx - k, n_ctx - k - 1, ch, t + 2).start()

        @pl.when(t == 6)
        def _():
            to_left(n_ctx - k, n_ctx - k - 1, ch, 7).start()

        attend(k, ch, n_ctx - k, ch)
        return 0

    lax.fori_loop(1, 7, ring, 0)

    def rs_right(step, ch):
        return send(part(po, step - 1, ch), part(pin_l, step - 1, ch),
                    rs_ss.at[0, step - 1, ch], rs_rs.at[0, step - 1, ch], "ctx", right)

    def rs_left(step, ch):
        return send(part(po, 3 + step, ch), part(pin_r, step - 1, ch),
                    rs_ss.at[1, step - 1, ch], rs_rs.at[1, step - 1, ch], "ctx", left)

    def pass_right(step, ch, add):
        total = part(acc, 3 + step, ch)[...]
        if add:
            rs_right(step - 1, ch).wait_recv()
            total = total + part(pin_l, step - 2, ch)[...].astype(F32)
        part(po, step - 1, ch)[...] = total.astype(BF)
        rs_right(step, ch).start()

    def pass_left(step, ch, add):
        total = part(acc, 5 - step, ch)[...]
        if add:
            rs_left(step - 1, ch).wait_recv()
            total = total + part(pin_r, step - 2, ch)[...].astype(F32)
        part(po, 3 + step, ch)[...] = total.astype(BF)
        rs_left(step, ch).start()

    pass_right(2, 1, False)
    pass_left(2, 0, False)
    to_right(0, 4, 0, 7).wait_recv()
    to_left(0, 4, 1, 7).wait_recv()
    attend(4, 0, 4, 1)
    pass_right(1, 0, False)
    pass_left(1, 1, False)

    arrived(sg, rg, sg_ss, sg_rs)
    gate_v[...] = dot(unhot_v[...], rg[...].reshape(slot_total, width))

    pass_right(3, 1, True)
    pass_left(3, 0, True)
    pass_right(2, 0, True)
    pass_left(2, 1, True)
    pass_right(4, 1, True)
    pass_left(4, 0, True)
    pass_right(3, 0, True)
    pass_left(3, 1, True)
    pass_right(4, 0, True)
    pass_left(4, 1, True)

    def xg_copy(k, ch):
        return send(part(g_all, 0, ch), part(g_all, k, ch), xg_ss.at[k, ch], xg_rs.at[k, ch],
                    "head", lax.rem(h + k, n_head))

    for ch in (0, 1):
        rs_right(4, ch).wait_recv()
        rs_left(4, ch).wait_recv()
        attended = part(acc, 0, ch)[...] + part(pin_l, 3, ch)[...].astype(F32) + part(pin_r, 3, ch)[...].astype(F32)
        rows = slice(ch * half, (ch + 1) * half)
        part(g_all, 0, ch)[...] = (attended * gate_v[rows]).astype(BF)
        for k in (2, 1, 3):
            xg_copy(k, ch).start()

    for k in range(1, n_head):
        wx_copy(k).wait_recv()
    for ch in (0, 1):
        total = dot(part(g_all, 0, ch)[...], wx[0])
        for k in (1, 3, 2):
            xg_copy(k, ch).wait_recv()
            total = total + dot(part(g_all, k, ch)[...], wx[k])
        out_ref[ch * half:(ch + 1) * half] = total.astype(BF)

    drained(req_out, req_in, req_ss, req_rs)
    drained(sq, rq, sq_ss, sq_rs)
    drained(sg, rg, sg_ss, sg_rs)
    for k in range(1, n_head):
        wx_copy(k).wait_send()
        for ch in (0, 1):
            xg_copy(k, ch).wait_send()
    for number in range(1, 8):
        to_right(0, 1, 0, number).wait_send()
        to_left(0, 1, 0, number).wait_send()
    for step in range(1, 5):
        for ch in (0, 1):
            if step > 1 or ch == 0:
                rs_right(step, ch).wait_send()
            if step > 1 or ch == 1:
                rs_left(step, ch).wait_send()


def per_device(catalog, cand_owner, cand_row, hist_len, proj_weight, keys, values, out_weight):
    n_user, n_ctx, n_head = (lax.axis_size(a) for a in ("user", "ctx", "head"))
    cand = cand_row.shape[1]
    rows, model = catalog.shape
    hist, width = keys.shape[1:]
    slots = n_user * SLOTS
    any_space = pl.BlockSpec(memory_space=pl.ANY)
    vmem = pl.BlockSpec(memory_space=pltpu.VMEM)
    dma = pltpu.SemaphoreType.DMA
    piece = (n_user, SLOTS, width)
    ranked = pl.pallas_call(
        functools.partial(kernel, n_user, n_ctx, n_head),
        out_shape=jax.ShapeDtypeStruct((cand, width), BF),
        in_specs=[any_space, vmem, vmem, vmem, any_space, any_space, any_space, any_space],
        out_specs=vmem,
        scratch_shapes=[
            pltpu.VMEM((rows, model), BF),
            pltpu.VMEM((2, model, width), BF),
            pltpu.VMEM((hist, width), BF),
            pltpu.VMEM((hist, width), BF),
            pltpu.VMEM((width, model), BF),
            pltpu.VMEM((n_user, 1, 128), jnp.int32),
            pltpu.VMEM((n_user, 1, 128), jnp.int32),
            pltpu.VMEM((rows, width), BF),
            pltpu.VMEM((rows, width), BF),
            pltpu.VMEM((slots, rows), BF),
            pltpu.VMEM((cand, slots), BF),
            pltpu.VMEM(piece, BF),
            pltpu.VMEM(piece, BF),
            pltpu.VMEM(piece, BF),
            pltpu.VMEM(piece, BF),
            pltpu.VMEM((n_ctx, cand, width), BF),
            pltpu.VMEM((n_ctx, cand, width), F32),
            pltpu.VMEM((8, cand, width), BF),
            pltpu.VMEM((4, cand, width), BF),
            pltpu.VMEM((4, cand, width), BF),
            pltpu.VMEM((cand, width), F32),
            pltpu.VMEM((n_head, cand, width), BF),
            pltpu.VMEM((n_head, width, width), BF),
            dma((5,)),
            dma((n_user,)), dma((n_user,)),
            dma((n_user,)), dma((n_user,)),
            dma((n_user,)), dma((n_user,)),
            dma((2, 8)), dma((2, 8)),
            dma((2, 4, 2)), dma((2, 4, 2)),
            dma((n_head,)), dma((n_head,)),
            dma((n_head, 2)), dma((n_head, 2)),
        ],
        compiler_params=pltpu.CompilerParams(
            collective_id=0, has_side_effects=True, vmem_limit_bytes=40 * 2**20
        ),
        name="rank_items",
    )(
        catalog,
        cand_owner.reshape(1, cand),
        cand_row,
        hist_len.reshape(1, 1),
        jnp.transpose(proj_weight, (1, 0, 2)),
        keys.reshape(hist, width),
        values.reshape(hist, width),
        out_weight,
    )
    return ranked.reshape(1, cand, width)


def solution(mesh):
    return jax.shard_map(
        per_device,
        mesh=mesh,
        in_specs=(
            P("user", None),
            P("user", "ctx", None),
            P("user", "ctx"),
            P("user"),
            P(None, None, "head"),
            P("user", "ctx", "head"),
            P("user", "ctx", "head"),
            P("head", None),
        ),
        out_specs=P("user", "ctx", "head"),
        check_vma=False,
    )
```

```python
import functools

import jax
import jax.numpy as jnp
from jax import lax
from jax.experimental import pallas as pl
from jax.experimental.pallas import tpu as pltpu
from jax.sharding import PartitionSpec as P

HEAD = 128
MESH = pl.DeviceIdType.MESH
BF = jnp.bfloat16
F32 = jnp.float32
SLOTS = 32
KEY_STEP = 768
CHUNKS = 4


def send(src, dst, ssem, rsem, axis, index):
    return pltpu.make_async_remote_copy(
        src_ref=src, dst_ref=dst, send_sem=ssem, recv_sem=rsem,
        device_id={axis: index}, device_id_type=MESH,
    )


def column(row, lanes):
    tall = jnp.broadcast_to(row, (128, row.shape[1])).T
    return jnp.concatenate([tall] * (lanes // 128), axis=1)


def silu(v):
    return v / (1.0 + jnp.exp(-v))


def dot(a, b):
    return jnp.dot(a, b, preferred_element_type=F32)


def dot_t(a, b):
    return lax.dot_general(a, b, (((1,), (1,)), ((), ())), preferred_element_type=F32)


def kernel(
    n_user, n_ctx, n_head,
    cat_hbm, owner_ref, row_ref, len_ref, w_hbm, key_hbm, val_hbm, wout_hbm,
    out_ref,
    cat_v, w_pairs, w_v, key_v, val_v, wout_v,
    req_out, req_in, tab_q, tab_g, hot_v, unhot_v, sq, sg, rq, rg,
    q_all, acc, po, pin_l, pin_r, gate_v, g_all, wx,
    load_sem, req_ss, req_rs, sq_ss, sq_rs, sg_ss, sg_rs,
    ag_ss, ag_rs, rs_ss, rs_rs, wx_ss, wx_rs, xg_ss, xg_rs,
):
    u = lax.axis_index("user")
    c = lax.axis_index("ctx")
    h = lax.axis_index("head")
    right, left = lax.rem(c + 1, n_ctx), lax.rem(c + n_ctx - 1, n_ctx)
    cand = owner_ref.shape[1]
    half = cand // 2
    chunk = cand // CHUNKS
    hist = key_v.shape[0]
    width = key_v.shape[1]
    model = cat_v.shape[1]
    slot_total = n_user * SLOTS

    barrier = pltpu.get_barrier_semaphore()

    def greet(d, _):
        pl.semaphore_signal(barrier, inc=1, device_id={"user": lax.rem(u + d, n_user)}, device_id_type=MESH)
        return 0

    lax.fori_loop(1, n_user, greet, 0)
    for other in (left, right):
        pl.semaphore_signal(barrier, inc=1, device_id={"ctx": other}, device_id_type=MESH)
    for k in range(1, n_head):
        pl.semaphore_signal(barrier, inc=1, device_id={"head": lax.rem(h + k, n_head)}, device_id_type=MESH)

    loads = [
        pltpu.make_async_copy(a, b, load_sem.at[i])
        for i, (a, b) in enumerate(
            ((cat_hbm, cat_v), (w_hbm, w_pairs), (wout_hbm, wout_v), (key_hbm, key_v), (val_hbm, val_v))
        )
    ]
    for copy in loads:
        copy.start()

    owner = owner_ref[...].astype(F32)
    owner_col = column(owner, cand)
    first = lax.broadcasted_iota(jnp.int32, (cand, cand), 0)
    second = lax.broadcasted_iota(jnp.int32, (cand, cand), 1)
    before = jnp.where((owner_col == owner) & (first < second), 1.0, 0.0)
    rank = jnp.sum(before, axis=0, keepdims=True)
    place_col = column(owner * SLOTS + rank, slot_total)
    slot_lane = lax.broadcasted_iota(jnp.int32, (cand, slot_total), 1).astype(F32)
    unhot_v[...] = jnp.where(place_col == slot_lane, 1.0, 0.0).astype(BF)
    rank_col = place_col[:, :128] - owner_col[:, :128] * SLOTS
    shift = (lax.rem(u, 4) * SLOTS).astype(F32)
    rank_hot = jnp.where(rank_col + shift == slot_lane[:, :128], 1.0, 0.0).astype(BF)
    wanted = row_ref[...]
    shard = lax.broadcasted_iota(jnp.int32, (n_user, cand), 0)
    mine = owner_ref[...] == shard
    high = jnp.where(mine, lax.shift_right_logical(wanted, 4).astype(F32), 0.0)
    low = jnp.where(mine, (wanted & 15).astype(F32), 0.0)
    asked = dot(jnp.concatenate([high, low], axis=0).astype(BF), rank_hot)
    asked = (asked[:n_user] * 16.0 + asked[n_user:]).astype(jnp.int32)
    for s in range(n_user):
        req_out[s] = asked[s:s + 1]

    pl.semaphore_wait(barrier, n_user - 1 + 2 + n_head - 1)

    def exchange(src, dst, ssem, rsem):
        def start(d, _):
            to = lax.rem(u + d, n_user)
            send(src.at[to], dst.at[u], ssem.at[d], rsem.at[d], "user", to).start()
            return 0

        lax.fori_loop(1, n_user, start, 0)
        dst[u] = src[u]

    def arrived(src, dst, ssem, rsem):
        def wait(d, _):
            origin = lax.rem(u + n_user - d, n_user)
            send(src.at[0], dst.at[origin], ssem.at[d], rsem.at[d], "user", lax.rem(u + d, n_user)).wait_recv()
            return 0

        lax.fori_loop(1, n_user, wait, 0)

    def drained(src, dst, ssem, rsem):
        def wait(d, _):
            to = lax.rem(u + d, n_user)
            send(src.at[to], dst.at[u], ssem.at[d], rsem.at[d], "user", to).wait_send()
            return 0

        lax.fori_loop(1, n_user, wait, 0)

    exchange(req_out, req_in, req_ss, req_rs)

    loads[0].wait()
    loads[1].wait()
    to = lax.broadcasted_iota(jnp.int32, (256, 256), 0)
    source = jnp.where(to < 128, 2 * to, 2 * to - 255)
    split = jnp.where(source == lax.broadcasted_iota(jnp.int32, (256, 256), 1), 1.0, 0.0).astype(BF)
    pairs = w_pairs[...].reshape(2 * model, width)
    for i in range(model // 128):
        apart = dot(split, pairs[256 * i:256 * (i + 1)]).astype(BF)
        w_v[0, 128 * i:128 * (i + 1)] = apart[:128]
        w_v[1, 128 * i:128 * (i + 1)] = apart[128:]
    tab_q[...] = silu(dot(cat_v[...], w_v[0])).astype(BF)
    tab_g[...] = silu(dot(cat_v[...], w_v[1])).astype(BF)

    loads[2].wait()

    def wx_copy(k):
        to = lax.rem(h + k, n_head)
        cols = pl.ds(pl.multiple_of(to * width, width), width)
        return send(wout_v.at[:, cols], wx.at[k], wx_ss.at[k], wx_rs.at[k], "head", to)

    for k in range(1, n_head):
        wx_copy(k).start()
    wx[0] = wout_v[:, pl.ds(pl.multiple_of(h * width, width), width)]

    acc[...] = jnp.zeros_like(acc)
    arrived(req_out, req_in, req_ss, req_rs)
    row_lane = lax.broadcasted_iota(jnp.int32, (128, cat_v.shape[0]), 1).astype(F32)
    for g in range(n_user // 4):
        ids = req_in[4 * g] + req_in[4 * g + 1] + req_in[4 * g + 2] + req_in[4 * g + 3]
        hot = jnp.where(column(ids.astype(F32), cat_v.shape[0]) == row_lane, 1.0, 0.0)
        hot_v[128 * g:128 * (g + 1)] = hot.astype(BF)
    sq[...] = dot(hot_v[...], tab_q[...]).astype(BF).reshape(sq.shape)
    exchange(sq, rq, sq_ss, sq_rs)

    loads[3].wait()
    loads[4].wait()
    length = len_ref[0]
    place = lax.broadcasted_iota(jnp.int32, (hist, width), 0) + c * hist
    val_v[...] = jnp.where(place < length, val_v[...].astype(F32), 0.0).astype(BF)
    scale = HEAD ** -0.5
    arg_scale = 0.5 * scale
    out_scale = (0.5 * scale) / jnp.full((1, KEY_STEP), length, jnp.int32).astype(F32)

    arrived(sq, rq, sq_ss, sq_rs)
    q_all[0] = dot(unhot_v[...], rq[...].reshape(slot_total, width)).astype(BF)

    def part(ref, block, ch):
        return ref.at[block, pl.ds(pl.multiple_of(ch * chunk, chunk), chunk)]

    def half_of(ref, block, j):
        return ref.at[block, pl.ds(pl.multiple_of(j * half, half), half)]

    def to_right(src_block, dst_block, ch, number):
        return send(part(q_all, src_block, ch), part(q_all, dst_block, ch),
                    ag_ss.at[0, number], ag_rs.at[0, number], "ctx", right)

    def to_left(src_block, dst_block, ch, number):
        return send(part(q_all, src_block, ch), part(q_all, dst_block, ch),
                    ag_ss.at[1, number], ag_rs.at[1, number], "ctx", left)

    for i in range(CHUNKS):
        to_right(0, 1, i, i).start()
        to_left(0, n_ctx - 1, CHUNKS - 1 - i, i).start()

    def attend(block_a, half_a, block_b, half_b, piece):
        queries = jnp.concatenate([half_of(q_all, block_a, half_a)[...], half_of(q_all, block_b, half_b)[...]], axis=0)
        rows = pl.ds(pl.multiple_of(piece * KEY_STEP, KEY_STEP), KEY_STEP)
        terms = []
        for n in range(width // HEAD):
            cols = pl.ds(n * HEAD, HEAD)
            scores = dot_t(queries[:, n * HEAD:(n + 1) * HEAD], key_v[rows, cols])
            scaled = scores * out_scale
            weights = (scaled + scaled * jnp.tanh(scores * arg_scale)).astype(BF)
            terms.append(dot(weights, val_v[rows, cols]))
        mixed = jnp.concatenate(terms, axis=1)
        half_of(acc, block_a, half_a)[...] += mixed[:half]
        half_of(acc, block_b, half_b)[...] += mixed[half:]

    def rs_right(step, ch):
        return send(part(po, step - 1, ch), part(pin_l, step - 1, ch),
                    rs_ss.at[0, step - 1, ch], rs_rs.at[0, step - 1, ch], "ctx", right)

    def rs_left(step, ch):
        return send(part(po, 3 + step, ch), part(pin_r, step - 1, ch),
                    rs_ss.at[1, step - 1, ch], rs_rs.at[1, step - 1, ch], "ctx", left)

    def pass_right(step, ch, add):
        total = part(acc, 3 + step, ch)[...]
        if add:
            rs_right(step - 1, ch).wait_recv()
            total = total + part(pin_l, step - 2, ch)[...].astype(F32)
        part(po, step - 1, ch)[...] = total.astype(BF)
        rs_right(step, ch).start()

    def pass_left(step, ch, add):
        total = part(acc, 5 - step, ch)[...]
        if add:
            rs_left(step - 1, ch).wait_recv()
            total = total + part(pin_r, step - 2, ch)[...].astype(F32)
        part(po, 3 + step, ch)[...] = total.astype(BF)
        rs_left(step, ch).start()

    far = [(i, CHUNKS - 1 - i) for i in range(CHUNKS // 2)]
    near = [(CHUNKS // 2 + i, CHUNKS // 2 - 1 - i) for i in range(CHUNKS // 2)]

    def pass_on(step, pairs, add):
        for r, l in pairs:
            pass_right(step, r, add)
            pass_left(step, l, add)

    sg[...] = dot(hot_v[...], tab_g[...]).astype(BF).reshape(sg.shape)
    exchange(sg, rg, sg_ss, sg_rs)
    pieces = hist // KEY_STEP
    for p in range(pieces):
        attend(0, 0, 0, 1, p)

    last = 3 * CHUNKS + CHUNKS // 2
    quarter = CHUNKS // 4

    def ring(t, _):
        k = lax.div(t, CHUNKS) + 1
        i = lax.rem(t, CHUNKS)
        to_right(0, k, i, t).wait_recv()

        @pl.when(t < last - CHUNKS)
        def _():
            to_right(k, k + 1, i, t + CHUNKS).start()

        to_left(0, n_ctx - k, CHUNKS - 1 - i, t).wait_recv()

        @pl.when(t < last - CHUNKS)
        def _():
            to_left(n_ctx - k, n_ctx - k - 1, CHUNKS - 1 - i, t + CHUNKS).start()

        due = lax.div(t + 1, quarter) - 2
        task = lax.div(due, 2)

        @pl.when((lax.rem(t + 1, quarter) == 0) & (due >= 0) & (task < 6))
        def _():
            block = lax.div(task, 2) + 1
            j = lax.rem(task, 2)
            attend(block, j, n_ctx - block, 1 - j, lax.rem(due, 2))

        @pl.when(t == 11 * quarter - 1)
        def _():
            pass_on(2, near, False)

        return 0

    lax.fori_loop(0, last, ring, 0)
    for p in range(pieces):
        attend(4, 0, 4, 1, p)
    pass_on(1, far, False)

    arrived(sg, rg, sg_ss, sg_rs)
    gate_v[...] = dot(unhot_v[...], rg[...].reshape(slot_total, width))

    pass_on(3, near, True)
    pass_on(2, far, True)
    pass_on(4, near, True)
    pass_on(3, far, True)
    pass_on(4, far, True)

    def xg_copy(k, ch):
        return send(part(g_all, 0, ch), part(g_all, k, ch), xg_ss.at[k, ch], xg_rs.at[k, ch],
                    "head", lax.rem(h + k, n_head))

    order = [ch for pair in far for ch in pair]
    for ch in order:
        rs_right(4, ch).wait_recv()
        rs_left(4, ch).wait_recv()
        attended = part(acc, 0, ch)[...] + part(pin_l, 3, ch)[...].astype(F32) + part(pin_r, 3, ch)[...].astype(F32)
        rows = slice(ch * chunk, (ch + 1) * chunk)
        part(g_all, 0, ch)[...] = (attended * gate_v[rows]).astype(BF)
        for k in (2, 1, 3):
            xg_copy(k, ch).start()

    for k in range(1, n_head):
        wx_copy(k).wait_recv()
    for ch in order:
        total = dot(part(g_all, 0, ch)[...], wx[0])
        for k in (1, 3, 2):
            xg_copy(k, ch).wait_recv()
            total = total + dot(part(g_all, k, ch)[...], wx[k])
        out_ref[ch * chunk:(ch + 1) * chunk] = total.astype(BF)

    drained(req_out, req_in, req_ss, req_rs)
    drained(sq, rq, sq_ss, sq_rs)
    drained(sg, rg, sg_ss, sg_rs)
    for k in range(1, n_head):
        wx_copy(k).wait_send()
        for ch in range(CHUNKS):
            xg_copy(k, ch).wait_send()
    for number in range(last):
        to_right(0, 1, 0, number).wait_send()
        to_left(0, 1, 0, number).wait_send()
    for step in range(1, 5):
        for r, l in far if step == 1 else far + near:
            rs_right(step, r).wait_send()
            rs_left(step, l).wait_send()


def per_device(catalog, cand_owner, cand_row, hist_len, proj_weight, keys, values, out_weight):
    n_user, n_ctx, n_head = (lax.axis_size(a) for a in ("user", "ctx", "head"))
    cand = cand_row.shape[1]
    rows, model = catalog.shape
    hist, width = keys.shape[1:]
    slots = n_user * SLOTS
    any_space = pl.BlockSpec(memory_space=pltpu.HBM)
    vmem = pl.BlockSpec(memory_space=pltpu.VMEM)
    smem = pl.BlockSpec(memory_space=pltpu.SMEM)
    dma = pltpu.SemaphoreType.DMA
    piece = (n_user, SLOTS, width)
    ranked = pl.pallas_call(
        functools.partial(kernel, n_user, n_ctx, n_head),
        out_shape=jax.ShapeDtypeStruct((cand, width), BF),
        in_specs=[any_space, vmem, vmem, smem, any_space, any_space, any_space, any_space],
        out_specs=vmem,
        scratch_shapes=[
            pltpu.VMEM((rows, model), BF),
            pltpu.VMEM((model, 2, width), BF),
            pltpu.VMEM((2, model, width), BF),
            pltpu.VMEM((hist, width), BF),
            pltpu.VMEM((hist, width), BF),
            pltpu.VMEM((width, model), BF),
            pltpu.VMEM((n_user, 1, 128), jnp.int32),
            pltpu.VMEM((n_user, 1, 128), jnp.int32),
            pltpu.VMEM((rows, width), BF),
            pltpu.VMEM((rows, width), BF),
            pltpu.VMEM((slots, rows), BF),
            pltpu.VMEM((cand, slots), BF),
            pltpu.VMEM(piece, BF),
            pltpu.VMEM(piece, BF),
            pltpu.VMEM(piece, BF),
            pltpu.VMEM(piece, BF),
            pltpu.VMEM((n_ctx, cand, width), BF),
            pltpu.VMEM((n_ctx, cand, width), F32),
            pltpu.VMEM((8, cand, width), BF),
            pltpu.VMEM((4, cand, width), BF),
            pltpu.VMEM((4, cand, width), BF),
            pltpu.VMEM((cand, width), F32),
            pltpu.VMEM((n_head, cand, width), BF),
            pltpu.VMEM((n_head, width, width), BF),
            dma((5,)),
            dma((n_user,)), dma((n_user,)),
            dma((n_user,)), dma((n_user,)),
            dma((n_user,)), dma((n_user,)),
            dma((2, 4 * CHUNKS)), dma((2, 4 * CHUNKS)),
            dma((2, 4, CHUNKS)), dma((2, 4, CHUNKS)),
            dma((n_head,)), dma((n_head,)),
            dma((n_head, CHUNKS)), dma((n_head, CHUNKS)),
        ],
        compiler_params=pltpu.CompilerParams(
            collective_id=0, has_side_effects=True, vmem_limit_bytes=60 * 2**20
        ),
        name="rank_items",
    )(
        catalog,
        cand_owner.reshape(1, cand),
        cand_row,
        hist_len,
        proj_weight,
        keys.reshape(hist, width),
        values.reshape(hist, width),
        out_weight,
    )
    return ranked.reshape(1, cand, width)


def solution(mesh):
    return jax.shard_map(
        per_device,
        mesh=mesh,
        in_specs=(
            P("user", None),
            P("user", "ctx", None),
            P("user", "ctx"),
            P("user"),
            P(None, None, "head"),
            P("user", "ctx", "head"),
            P("user", "ctx", "head"),
            P("head", None),
        ),
        out_specs=P("user", "ctx", "head"),
        check_vma=False,
    )
```

```python
import functools

import jax
import jax.numpy as jnp
from jax import lax
from jax.experimental import pallas as pl
from jax.experimental.pallas import tpu as pltpu
from jax.sharding import PartitionSpec as P

HEAD = 128
MESH = pl.DeviceIdType.MESH
BF = jnp.bfloat16
F32 = jnp.float32
SLOTS = 32
KEY_STEP = 768
CHUNKS = 4


def send(src, dst, ssem, rsem, axis, index):
    return pltpu.make_async_remote_copy(
        src_ref=src, dst_ref=dst, send_sem=ssem, recv_sem=rsem,
        device_id={axis: index}, device_id_type=MESH,
    )


def column(row, lanes):
    tall = jnp.broadcast_to(row, (128, row.shape[1])).T
    return jnp.concatenate([tall] * (lanes // 128), axis=1)


def silu(v):
    return v / (1.0 + jnp.exp(-v))


def dot(a, b):
    return jnp.dot(a, b, preferred_element_type=F32)


def dot_t(a, b):
    return lax.dot_general(a, b, (((1,), (1,)), ((), ())), preferred_element_type=F32)


def kernel(
    n_user, n_ctx, n_head,
    cat_hbm, owner_ref, row_ref, len_ref, w_hbm, key_hbm, val_hbm, wout_hbm,
    out_ref,
    cat_v, w_pairs, w_v, key_v, val_v, wout_v,
    req_out, req_in, tab_q, tab_g, hot_v, unhot_v, sq, sg, rq, rg,
    ids_f, req_f, hot_f, unhot_f, sf, rf,
    q_all, acc, po, pin_l, pin_r, gate_v, g_all, wx,
    load_sem, req_ss, req_rs, sq_ss, sq_rs, sf_ss, sf_rs, opp_ss, opp_rs, sg_ss, sg_rs,
    ag_ss, ag_rs, rs_ss, rs_rs, wx_ss, wx_rs, xg_ss, xg_rs,
):
    u = lax.axis_index("user")
    c = lax.axis_index("ctx")
    h = lax.axis_index("head")
    right, left = lax.rem(c + 1, n_ctx), lax.rem(c + n_ctx - 1, n_ctx)
    opposite = lax.rem(c + n_ctx // 2, n_ctx)
    cand = owner_ref.shape[1]
    half = cand // 2
    chunk = cand // CHUNKS
    hist = key_v.shape[0]
    width = key_v.shape[1]
    model = cat_v.shape[1]
    slot_total = n_user * SLOTS

    barrier = pltpu.get_barrier_semaphore()

    def greet(d, _):
        pl.semaphore_signal(barrier, inc=1, device_id={"user": lax.rem(u + d, n_user)}, device_id_type=MESH)
        return 0

    lax.fori_loop(1, n_user, greet, 0)
    for other in (left, right, opposite):
        pl.semaphore_signal(barrier, inc=1, device_id={"ctx": other}, device_id_type=MESH)
    for k in range(1, n_head):
        pl.semaphore_signal(barrier, inc=1, device_id={"head": lax.rem(h + k, n_head)}, device_id_type=MESH)

    loads = [
        pltpu.make_async_copy(a, b, load_sem.at[i])
        for i, (a, b) in enumerate(
            ((cat_hbm, cat_v), (w_hbm, w_pairs), (wout_hbm, wout_v), (key_hbm, key_v), (val_hbm, val_v))
        )
    ]
    for copy in loads:
        copy.start()

    slot_lane = lax.broadcasted_iota(jnp.int32, (cand, slot_total), 1).astype(F32)

    def places(ids):
        owner = ids.astype(F32)
        owner_col = column(owner, cand)
        first = lax.broadcasted_iota(jnp.int32, (cand, cand), 0)
        second = lax.broadcasted_iota(jnp.int32, (cand, cand), 1)
        before = jnp.where((owner_col == owner) & (first < second), 1.0, 0.0)
        rank = jnp.sum(before, axis=0, keepdims=True)
        place_col = column(owner * SLOTS + rank, slot_total)
        return owner_col, place_col, jnp.where(place_col == slot_lane, 1.0, 0.0).astype(BF)

    owner_col, place_col, unhot_v[...] = places(owner_ref[...])
    rank_col = place_col[:, :128] - owner_col[:, :128] * SLOTS
    shift = (lax.rem(u, 4) * SLOTS).astype(F32)
    rank_hot = jnp.where(rank_col + shift == slot_lane[:, :128], 1.0, 0.0).astype(BF)
    wanted = row_ref[...]
    shard = lax.broadcasted_iota(jnp.int32, (n_user, cand), 0)
    mine = owner_ref[...] == shard
    high = jnp.where(mine, lax.shift_right_logical(wanted, 4).astype(F32), 0.0)
    low = jnp.where(mine, (wanted & 15).astype(F32), 0.0)
    asked = dot(jnp.concatenate([high, low], axis=0).astype(BF), rank_hot)
    asked = (asked[:n_user] * 16.0 + asked[n_user:]).astype(jnp.int32)
    for s in range(n_user):
        req_out[s] = asked[s:s + 1]

    pl.semaphore_wait(barrier, n_user - 1 + 3 + n_head - 1)

    def exchange(src, dst, ssem, rsem):
        def start(d, _):
            to = lax.rem(u + d, n_user)
            send(src.at[to], dst.at[u], ssem.at[d], rsem.at[d], "user", to).start()
            return 0

        lax.fori_loop(1, n_user, start, 0)
        dst[u] = src[u]

    def arrived(src, dst, ssem, rsem):
        def wait(d, _):
            origin = lax.rem(u + n_user - d, n_user)
            send(src.at[0], dst.at[origin], ssem.at[d], rsem.at[d], "user", lax.rem(u + d, n_user)).wait_recv()
            return 0

        lax.fori_loop(1, n_user, wait, 0)

    def drained(src, dst, ssem, rsem):
        def wait(d, _):
            to = lax.rem(u + d, n_user)
            send(src.at[to], dst.at[u], ssem.at[d], rsem.at[d], "user", to).wait_send()
            return 0

        lax.fori_loop(1, n_user, wait, 0)

    ids_copy = send(owner_ref, ids_f, opp_ss.at[0], opp_rs.at[0], "ctx", opposite)
    req_copy = send(req_in, req_f, opp_ss.at[1], opp_rs.at[1], "ctx", opposite)
    exchange(req_out, req_in, req_ss, req_rs)
    ids_copy.start()

    loads[0].wait()
    loads[1].wait()
    to = lax.broadcasted_iota(jnp.int32, (256, 256), 0)
    source = jnp.where(to < 128, 2 * to, 2 * to - 255)
    split = jnp.where(source == lax.broadcasted_iota(jnp.int32, (256, 256), 1), 1.0, 0.0).astype(BF)
    pairs = w_pairs[...].reshape(2 * model, width)
    for i in range(model // 128):
        apart = dot(split, pairs[256 * i:256 * (i + 1)]).astype(BF)
        w_v[0, 128 * i:128 * (i + 1)] = apart[:128]
        w_v[1, 128 * i:128 * (i + 1)] = apart[128:]
    tab_q[...] = silu(dot(cat_v[...], w_v[0])).astype(BF)
    tab_g[...] = silu(dot(cat_v[...], w_v[1])).astype(BF)

    loads[2].wait()

    def wx_copy(k):
        to = lax.rem(h + k, n_head)
        cols = pl.ds(pl.multiple_of(to * width, width), width)
        return send(wout_v.at[:, cols], wx.at[k], wx_ss.at[k], wx_rs.at[k], "head", to)

    for k in range(1, n_head):
        wx_copy(k).start()
    wx[0] = wout_v[:, pl.ds(pl.multiple_of(h * width, width), width)]

    acc[...] = jnp.zeros_like(acc)
    arrived(req_out, req_in, req_ss, req_rs)
    req_copy.start()
    row_lane = lax.broadcasted_iota(jnp.int32, (128, cat_v.shape[0]), 1).astype(F32)

    def pick(requests, hot_ref):
        for g in range(n_user // 4):
            ids = requests[4 * g] + requests[4 * g + 1] + requests[4 * g + 2] + requests[4 * g + 3]
            hot = jnp.where(column(ids.astype(F32), cat_v.shape[0]) == row_lane, 1.0, 0.0)
            hot_ref[128 * g:128 * (g + 1)] = hot.astype(BF)

    pick(req_in, hot_v)
    sq[...] = dot(hot_v[...], tab_q[...]).astype(BF).reshape(sq.shape)
    exchange(sq, rq, sq_ss, sq_rs)

    req_copy.wait_recv()
    pick(req_f, hot_f)
    sf[...] = dot(hot_f[...], tab_q[...]).astype(BF).reshape(sf.shape)
    exchange(sf, rf, sf_ss, sf_rs)

    arrived(sq, rq, sq_ss, sq_rs)
    q_all[0] = dot(unhot_v[...], rq[...].reshape(slot_total, width)).astype(BF)

    def part(ref, block, ch):
        return ref.at[block, pl.ds(pl.multiple_of(ch * chunk, chunk), chunk)]

    def half_of(ref, block, j):
        return ref.at[block, pl.ds(pl.multiple_of(j * half, half), half)]

    def to_right(src_block, dst_block, ch, number):
        return send(part(q_all, src_block, ch), part(q_all, dst_block, ch),
                    ag_ss.at[0, number], ag_rs.at[0, number], "ctx", right)

    def to_left(src_block, dst_block, ch, number):
        return send(part(q_all, src_block, ch), part(q_all, dst_block, ch),
                    ag_ss.at[1, number], ag_rs.at[1, number], "ctx", left)

    for i in range(CHUNKS):
        to_right(0, 1, i, i).start()
        to_left(0, n_ctx - 1, CHUNKS - 1 - i, i).start()

    ids_copy.wait_recv()
    unhot_f[...] = places(ids_f[...])[2]

    loads[3].wait()
    loads[4].wait()
    length = len_ref[0]
    place = lax.broadcasted_iota(jnp.int32, (hist, width), 0) + c * hist
    val_v[...] = jnp.where(place < length, val_v[...].astype(F32), 0.0).astype(BF)
    scale = HEAD ** -0.5
    arg_scale = 0.5 * scale
    out_scale = (0.5 * scale) / jnp.full((1, KEY_STEP), length, jnp.int32).astype(F32)

    def attend(block_a, half_a, block_b, half_b, piece):
        queries = jnp.concatenate([half_of(q_all, block_a, half_a)[...], half_of(q_all, block_b, half_b)[...]], axis=0)
        rows = pl.ds(pl.multiple_of(piece * KEY_STEP, KEY_STEP), KEY_STEP)
        terms = []
        for n in range(width // HEAD):
            cols = pl.ds(n * HEAD, HEAD)
            scores = dot_t(queries[:, n * HEAD:(n + 1) * HEAD], key_v[rows, cols])
            scaled = scores * out_scale
            weights = (scaled + scaled * jnp.tanh(scores * arg_scale)).astype(BF)
            terms.append(dot(weights, val_v[rows, cols]))
        mixed = jnp.concatenate(terms, axis=1)
        half_of(acc, block_a, half_a)[...] += mixed[:half]
        half_of(acc, block_b, half_b)[...] += mixed[half:]

    def rs_right(step, ch):
        return send(part(po, step - 1, ch), part(pin_l, step - 1, ch),
                    rs_ss.at[0, step - 1, ch], rs_rs.at[0, step - 1, ch], "ctx", right)

    def rs_left(step, ch):
        return send(part(po, 3 + step, ch), part(pin_r, step - 1, ch),
                    rs_ss.at[1, step - 1, ch], rs_rs.at[1, step - 1, ch], "ctx", left)

    def pass_right(step, ch, add):
        total = part(acc, 3 + step, ch)[...]
        if add:
            rs_right(step - 1, ch).wait_recv()
            total = total + part(pin_l, step - 2, ch)[...].astype(F32)
        part(po, step - 1, ch)[...] = total.astype(BF)
        rs_right(step, ch).start()

    def pass_left(step, ch, add):
        total = part(acc, 5 - step, ch)[...]
        if add:
            rs_left(step - 1, ch).wait_recv()
            total = total + part(pin_r, step - 2, ch)[...].astype(F32)
        part(po, 3 + step, ch)[...] = total.astype(BF)
        rs_left(step, ch).start()

    far = [(i, CHUNKS - 1 - i) for i in range(CHUNKS // 2)]
    near = [(CHUNKS // 2 + i, CHUNKS // 2 - 1 - i) for i in range(CHUNKS // 2)]

    def pass_on(step, pairs, add):
        for r, l in pairs:
            pass_right(step, r, add)
            pass_left(step, l, add)

    pieces = hist // KEY_STEP
    for p in range(pieces):
        attend(0, 0, 0, 1, p)

    def come(t):
        k = lax.div(t, CHUNKS) + 1
        i = lax.rem(t, CHUNKS)
        return k, i, to_right(0, k, i, t), to_left(0, n_ctx - k, CHUNKS - 1 - i, t)

    last = 3 * CHUNKS
    quarter = CHUNKS // 4

    def ring(t, _):
        k, i, from_left, from_right = come(t)
        from_left.wait_recv()
        to_right(k, k + 1, i, t + CHUNKS).start()
        from_right.wait_recv()
        to_left(n_ctx - k, n_ctx - k - 1, CHUNKS - 1 - i, t + CHUNKS).start()
        due = lax.div(t + 1, quarter) - 2
        task = lax.div(due, 2)

        @pl.when((lax.rem(t + 1, quarter) == 0) & (due >= 0) & (task < 3))
        def _():
            block = lax.div(task, 2) + 1
            j = lax.rem(task, 2)
            attend(block, j, n_ctx - block, 1 - j, lax.rem(due, 2))

        return 0

    lax.fori_loop(0, last - CHUNKS, ring, 0)

    arrived(sf, rf, sf_ss, sf_rs)
    q_all[4] = dot(unhot_f[...], rf[...].reshape(slot_total, width)).astype(BF)

    def attend_piece(block_a, half_a, block_b, half_b):
        def body(p, _):
            attend(block_a, half_a, block_b, half_b, p)
            return 0

        lax.fori_loop(0, pieces, body, 0)

    attend_piece(4, 0, 4, 1)
    pass_on(1, far, False)
    sg[...] = dot(hot_v[...], tab_g[...]).astype(BF).reshape(sg.shape)
    exchange(sg, rg, sg_ss, sg_rs)

    def land(t, _):
        k, i, from_left, from_right = come(t)
        from_left.wait_recv()
        from_right.wait_recv()
        return 0

    lax.fori_loop(last - CHUNKS, last - CHUNKS // 2, land, 0)
    attend_piece(3, 0, 5, 1)
    pass_on(2, near, False)
    lax.fori_loop(last - CHUNKS // 2, last, land, 0)
    attend_piece(3, 1, 5, 0)
    pass_on(2, far, True)
    attend_piece(2, 1, 6, 0)
    pass_on(3, near, True)
    pass_on(3, far, True)
    pass_on(4, near, True)
    pass_on(4, far, True)
    arrived(sg, rg, sg_ss, sg_rs)
    gate_v[...] = dot(unhot_v[...], rg[...].reshape(slot_total, width))

    def xg_copy(k, ch):
        return send(part(g_all, 0, ch), part(g_all, k, ch), xg_ss.at[k, ch], xg_rs.at[k, ch],
                    "head", lax.rem(h + k, n_head))

    order = [ch for pair in far for ch in pair]
    for ch in order:
        rs_right(4, ch).wait_recv()
        rs_left(4, ch).wait_recv()
        attended = part(acc, 0, ch)[...] + part(pin_l, 3, ch)[...].astype(F32) + part(pin_r, 3, ch)[...].astype(F32)
        rows = slice(ch * chunk, (ch + 1) * chunk)
        part(g_all, 0, ch)[...] = (attended * gate_v[rows]).astype(BF)
        for k in (2, 1, 3):
            xg_copy(k, ch).start()

    for k in range(1, n_head):
        wx_copy(k).wait_recv()
    for ch in order:
        total = dot(part(g_all, 0, ch)[...], wx[0])
        for k in (1, 3, 2):
            xg_copy(k, ch).wait_recv()
            total = total + dot(part(g_all, k, ch)[...], wx[k])
        out_ref[ch * chunk:(ch + 1) * chunk] = total.astype(BF)

    drained(req_out, req_in, req_ss, req_rs)
    drained(sq, rq, sq_ss, sq_rs)
    drained(sf, rf, sf_ss, sf_rs)
    ids_copy.wait_send()
    req_copy.wait_send()
    drained(sg, rg, sg_ss, sg_rs)
    for k in range(1, n_head):
        wx_copy(k).wait_send()
        for ch in range(CHUNKS):
            xg_copy(k, ch).wait_send()
    for number in range(last):
        to_right(0, 1, 0, number).wait_send()
        to_left(0, 1, 0, number).wait_send()
    for step in range(1, 5):
        for r, l in far if step == 1 else far + near:
            rs_right(step, r).wait_send()
            rs_left(step, l).wait_send()


def per_device(catalog, cand_owner, cand_row, hist_len, proj_weight, keys, values, out_weight):
    n_user, n_ctx, n_head = (lax.axis_size(a) for a in ("user", "ctx", "head"))
    cand = cand_row.shape[1]
    rows, model = catalog.shape
    hist, width = keys.shape[1:]
    slots = n_user * SLOTS
    any_space = pl.BlockSpec(memory_space=pltpu.HBM)
    vmem = pl.BlockSpec(memory_space=pltpu.VMEM)
    smem = pl.BlockSpec(memory_space=pltpu.SMEM)
    dma = pltpu.SemaphoreType.DMA
    piece = (n_user, SLOTS, width)
    ranked = pl.pallas_call(
        functools.partial(kernel, n_user, n_ctx, n_head),
        out_shape=jax.ShapeDtypeStruct((cand, width), BF),
        in_specs=[any_space, vmem, vmem, smem, any_space, any_space, any_space, any_space],
        out_specs=vmem,
        scratch_shapes=[
            pltpu.VMEM((rows, model), BF),
            pltpu.VMEM((model, 2, width), BF),
            pltpu.VMEM((2, model, width), BF),
            pltpu.VMEM((hist, width), BF),
            pltpu.VMEM((hist, width), BF),
            pltpu.VMEM((width, model), BF),
            pltpu.VMEM((n_user, 1, 128), jnp.int32),
            pltpu.VMEM((n_user, 1, 128), jnp.int32),
            pltpu.VMEM((rows, width), BF),
            pltpu.VMEM((rows, width), BF),
            pltpu.VMEM((slots, rows), BF),
            pltpu.VMEM((cand, slots), BF),
            pltpu.VMEM(piece, BF),
            pltpu.VMEM(piece, BF),
            pltpu.VMEM(piece, BF),
            pltpu.VMEM(piece, BF),
            pltpu.VMEM((1, cand), jnp.int32),
            pltpu.VMEM((n_user, 1, 128), jnp.int32),
            pltpu.VMEM((slots, rows), BF),
            pltpu.VMEM((cand, slots), BF),
            pltpu.VMEM(piece, BF),
            pltpu.VMEM(piece, BF),
            pltpu.VMEM((n_ctx, cand, width), BF),
            pltpu.VMEM((n_ctx, cand, width), F32),
            pltpu.VMEM((8, cand, width), BF),
            pltpu.VMEM((4, cand, width), BF),
            pltpu.VMEM((4, cand, width), BF),
            pltpu.VMEM((cand, width), F32),
            pltpu.VMEM((n_head, cand, width), BF),
            pltpu.VMEM((n_head, width, width), BF),
            dma((5,)),
            dma((n_user,)), dma((n_user,)),
            dma((n_user,)), dma((n_user,)),
            dma((n_user,)), dma((n_user,)),
            dma((2,)), dma((2,)),
            dma((n_user,)), dma((n_user,)),
            dma((2, 3 * CHUNKS)), dma((2, 3 * CHUNKS)),
            dma((2, 4, CHUNKS)), dma((2, 4, CHUNKS)),
            dma((n_head,)), dma((n_head,)),
            dma((n_head, CHUNKS)), dma((n_head, CHUNKS)),
        ],
        compiler_params=pltpu.CompilerParams(
            collective_id=0, has_side_effects=True, vmem_limit_bytes=60 * 2**20
        ),
        name="rank_items",
    )(
        catalog,
        cand_owner.reshape(1, cand),
        cand_row,
        hist_len,
        proj_weight,
        keys.reshape(hist, width),
        values.reshape(hist, width),
        out_weight,
    )
    return ranked.reshape(1, cand, width)


def solution(mesh):
    return jax.shard_map(
        per_device,
        mesh=mesh,
        in_specs=(
            P("user", None),
            P("user", "ctx", None),
            P("user", "ctx"),
            P("user"),
            P(None, None, "head"),
            P("user", "ctx", "head"),
            P("user", "ctx", "head"),
            P("head", None),
        ),
        out_specs=P("user", "ctx", "head"),
        check_vma=False,
    )
```

```python
import functools

import jax
import jax.numpy as jnp
from jax import lax
from jax.experimental import pallas as pl
from jax.experimental.pallas import tpu as pltpu
from jax.sharding import PartitionSpec as P

HEAD = 128
MESH = pl.DeviceIdType.MESH
BF = jnp.bfloat16
F32 = jnp.float32
SLOTS = 32
KEY_STEP = 768
CHUNKS = 4


def send(src, dst, ssem, rsem, axis, index):
    return pltpu.make_async_remote_copy(
        src_ref=src, dst_ref=dst, send_sem=ssem, recv_sem=rsem,
        device_id={axis: index}, device_id_type=MESH,
    )


def column(row, lanes):
    tall = jnp.broadcast_to(row, (128, row.shape[1])).T
    return jnp.concatenate([tall] * (lanes // 128), axis=1)


def silu(v):
    return v / (1.0 + jnp.exp(-v))


def dot(a, b):
    return jnp.dot(a, b, preferred_element_type=F32)


def dot_t(a, b):
    return lax.dot_general(a, b, (((1,), (1,)), ((), ())), preferred_element_type=F32)


def kernel(
    n_user, n_ctx, n_head,
    cat_hbm, owner_hbm, row_hbm, len_hbm, w_hbm, key_hbm, val_hbm, wout_hbm,
    out_ref,
    owner_ref, row_ref, len_ref, cat_v, w_pairs, w_v, key_v, val_v, wout_v,
    req_out, req_in, tab_q, tab_g, hot_v, unhot_v, sq, sg, rq, rg,
    ids_f, req_f, hot_f, unhot_f, sf, rf,
    q_all, acc, po, pin_l, pin_r, gate_v, g_all, wx,
    load_sem, req_ss, req_rs, sq_ss, sq_rs, sf_ss, sf_rs, opp_ss, opp_rs, sg_ss, sg_rs,
    ag_ss, ag_rs, rs_ss, rs_rs, wx_ss, wx_rs, xg_ss, xg_rs,
):
    u = lax.axis_index("user")
    c = lax.axis_index("ctx")
    h = lax.axis_index("head")
    right, left = lax.rem(c + 1, n_ctx), lax.rem(c + n_ctx - 1, n_ctx)
    opposite = lax.rem(c + n_ctx // 2, n_ctx)
    cand = owner_ref.shape[1]
    half = cand // 2
    chunk = cand // CHUNKS
    hist = key_v.shape[0]
    width = key_v.shape[1]
    model = cat_v.shape[1]
    slot_total = n_user * SLOTS

    barrier = pltpu.get_barrier_semaphore()

    def greet(d, _):
        pl.semaphore_signal(barrier, inc=1, device_id={"user": lax.rem(u + d, n_user)}, device_id_type=MESH)
        return 0

    lax.fori_loop(1, n_user, greet, 0)
    for other in (left, right, opposite):
        pl.semaphore_signal(barrier, inc=1, device_id={"ctx": other}, device_id_type=MESH)
    for k in range(1, n_head):
        pl.semaphore_signal(barrier, inc=1, device_id={"head": lax.rem(h + k, n_head)}, device_id_type=MESH)

    loads = [
        pltpu.make_async_copy(a, b, load_sem.at[i])
        for i, (a, b) in enumerate(
            ((cat_hbm, cat_v), (w_hbm, w_pairs), (wout_hbm, wout_v), (key_hbm, key_v), (val_hbm, val_v),
             (owner_hbm, owner_ref), (row_hbm, row_ref), (len_hbm, len_ref))
        )
    ]
    for copy in loads[5:] + loads[:5]:
        copy.start()
    loads[5].wait()
    loads[6].wait()

    slot_lane = lax.broadcasted_iota(jnp.int32, (cand, slot_total), 1).astype(F32)

    def places(ids):
        owner = ids.astype(F32)
        owner_col = column(owner, cand)
        first = lax.broadcasted_iota(jnp.int32, (cand, cand), 0)
        second = lax.broadcasted_iota(jnp.int32, (cand, cand), 1)
        before = jnp.where((owner_col == owner) & (first < second), 1.0, 0.0)
        rank = jnp.sum(before, axis=0, keepdims=True)
        place_col = column(owner * SLOTS + rank, slot_total)
        return owner_col, place_col, jnp.where(place_col == slot_lane, 1.0, 0.0).astype(BF)

    owner_col, place_col, unhot_v[...] = places(owner_ref[...])
    rank_col = place_col[:, :128] - owner_col[:, :128] * SLOTS
    shift = (lax.rem(u, 4) * SLOTS).astype(F32)
    rank_hot = jnp.where(rank_col + shift == slot_lane[:, :128], 1.0, 0.0).astype(BF)
    wanted = row_ref[...]
    shard = lax.broadcasted_iota(jnp.int32, (n_user, cand), 0)
    mine = owner_ref[...] == shard
    high = jnp.where(mine, lax.shift_right_logical(wanted, 4).astype(F32), 0.0)
    low = jnp.where(mine, (wanted & 15).astype(F32), 0.0)
    asked = dot(jnp.concatenate([high, low], axis=0).astype(BF), rank_hot)
    asked = (asked[:n_user] * 16.0 + asked[n_user:]).astype(jnp.int32)
    for s in range(n_user):
        req_out[s] = asked[s:s + 1]

    pl.semaphore_wait(barrier, n_user - 1 + 3 + n_head - 1)

    def exchange(src, dst, ssem, rsem):
        def start(d, _):
            to = lax.rem(u + d, n_user)
            send(src.at[to], dst.at[u], ssem.at[d], rsem.at[d], "user", to).start()
            return 0

        lax.fori_loop(1, n_user, start, 0)
        dst[u] = src[u]

    def arrived(src, dst, ssem, rsem):
        def wait(d, _):
            origin = lax.rem(u + n_user - d, n_user)
            send(src.at[0], dst.at[origin], ssem.at[d], rsem.at[d], "user", lax.rem(u + d, n_user)).wait_recv()
            return 0

        lax.fori_loop(1, n_user, wait, 0)

    def drained(src, dst, ssem, rsem):
        def wait(d, _):
            to = lax.rem(u + d, n_user)
            send(src.at[to], dst.at[u], ssem.at[d], rsem.at[d], "user", to).wait_send()
            return 0

        lax.fori_loop(1, n_user, wait, 0)

    ids_copy = send(owner_ref, ids_f, opp_ss.at[0], opp_rs.at[0], "ctx", opposite)
    req_copy = send(req_in, req_f, opp_ss.at[1], opp_rs.at[1], "ctx", opposite)
    exchange(req_out, req_in, req_ss, req_rs)
    ids_copy.start()

    loads[0].wait()
    loads[1].wait()
    to = lax.broadcasted_iota(jnp.int32, (256, 256), 0)
    source = jnp.where(to < 128, 2 * to, 2 * to - 255)
    split = jnp.where(source == lax.broadcasted_iota(jnp.int32, (256, 256), 1), 1.0, 0.0).astype(BF)
    pairs = w_pairs[...].reshape(2 * model, width)
    for i in range(model // 128):
        apart = dot(split, pairs[256 * i:256 * (i + 1)]).astype(BF)
        w_v[0, 128 * i:128 * (i + 1)] = apart[:128]
        w_v[1, 128 * i:128 * (i + 1)] = apart[128:]
    tab_q[...] = silu(dot(cat_v[...], w_v[0])).astype(BF)
    tab_g[...] = silu(dot(cat_v[...], w_v[1])).astype(BF)

    loads[2].wait()

    def wx_copy(k):
        to = lax.rem(h + k, n_head)
        cols = pl.ds(pl.multiple_of(to * width, width), width)
        return send(wout_v.at[:, cols], wx.at[k], wx_ss.at[k], wx_rs.at[k], "head", to)

    for k in range(1, n_head):
        wx_copy(k).start()
    wx[0] = wout_v[:, pl.ds(pl.multiple_of(h * width, width), width)]

    acc[...] = jnp.zeros_like(acc)
    arrived(req_out, req_in, req_ss, req_rs)
    req_copy.start()
    row_lane = lax.broadcasted_iota(jnp.int32, (128, cat_v.shape[0]), 1).astype(F32)

    def serve(requests, hot_ref, src, dst, ssem, rsem):
        def group(g, _):
            four = lax.rem(lax.div(u, 4) + g, n_user // 4) * 4
            ids = requests[four] + requests[four + 1] + requests[four + 2] + requests[four + 3]
            hot = jnp.where(column(ids.astype(F32), cat_v.shape[0]) == row_lane, 1.0, 0.0).astype(BF)
            hot_ref[pl.ds(pl.multiple_of(four * SLOTS, 128), 128)] = hot
            src[pl.ds(four, 4)] = dot(hot, tab_q[...]).astype(BF).reshape(4, SLOTS, width)
            for i in range(4):
                d = lax.rem(four + i - u + n_user, n_user)

                @pl.when(d > 0)
                def _():
                    send(src.at[four + i], dst.at[u], ssem.at[d], rsem.at[d], "user", four + i).start()

            return 0

        lax.fori_loop(1, n_user // 4 + 1, group, 0)
        dst[u] = src[u]

    serve(req_in, hot_v, sq, rq, sq_ss, sq_rs)

    req_copy.wait_recv()
    serve(req_f, hot_f, sf, rf, sf_ss, sf_rs)

    arrived(sq, rq, sq_ss, sq_rs)
    q_all[0] = dot(unhot_v[...], rq[...].reshape(slot_total, width)).astype(BF)

    def part(ref, block, ch):
        return ref.at[block, pl.ds(pl.multiple_of(ch * chunk, chunk), chunk)]

    def half_of(ref, block, j):
        return ref.at[block, pl.ds(pl.multiple_of(j * half, half), half)]

    def to_right(src_block, dst_block, ch, number):
        return send(part(q_all, src_block, ch), part(q_all, dst_block, ch),
                    ag_ss.at[0, number], ag_rs.at[0, number], "ctx", right)

    def to_left(src_block, dst_block, ch, number):
        return send(part(q_all, src_block, ch), part(q_all, dst_block, ch),
                    ag_ss.at[1, number], ag_rs.at[1, number], "ctx", left)

    for i in range(CHUNKS):
        to_right(0, 1, i, i).start()
        to_left(0, n_ctx - 1, CHUNKS - 1 - i, i).start()

    ids_copy.wait_recv()
    unhot_f[...] = places(ids_f[...])[2]

    loads[3].wait()
    loads[4].wait()
    loads[7].wait()
    length = len_ref[0]
    place = lax.broadcasted_iota(jnp.int32, (hist, width), 0) + c * hist
    val_v[...] = jnp.where(place < length, val_v[...].astype(F32), 0.0).astype(BF)
    scale = HEAD ** -0.5
    arg_scale = 0.5 * scale
    out_scale = (0.5 * scale) / jnp.full((1, KEY_STEP), length, jnp.int32).astype(F32)

    def attend(block_a, half_a, block_b, half_b, piece):
        queries = jnp.concatenate([half_of(q_all, block_a, half_a)[...], half_of(q_all, block_b, half_b)[...]], axis=0)
        rows = pl.ds(pl.multiple_of(piece * KEY_STEP, KEY_STEP), KEY_STEP)
        terms = []
        for n in range(width // HEAD):
            cols = pl.ds(n * HEAD, HEAD)
            scores = dot_t(queries[:, n * HEAD:(n + 1) * HEAD], key_v[rows, cols])
            scaled = scores * out_scale
            weights = (scaled + scaled * jnp.tanh(scores * arg_scale)).astype(BF)
            terms.append(dot(weights, val_v[rows, cols]))
        mixed = jnp.concatenate(terms, axis=1)
        half_of(acc, block_a, half_a)[...] += mixed[:half]
        half_of(acc, block_b, half_b)[...] += mixed[half:]

    def rs_right(step, ch):
        return send(part(po, step - 1, ch), part(pin_l, step - 1, ch),
                    rs_ss.at[0, step - 1, ch], rs_rs.at[0, step - 1, ch], "ctx", right)

    def rs_left(step, ch):
        return send(part(po, 3 + step, ch), part(pin_r, step - 1, ch),
                    rs_ss.at[1, step - 1, ch], rs_rs.at[1, step - 1, ch], "ctx", left)

    def pass_right(step, ch, add):
        total = part(acc, 3 + step, ch)[...]
        if add:
            rs_right(step - 1, ch).wait_recv()
            total = total + part(pin_l, step - 2, ch)[...].astype(F32)
        part(po, step - 1, ch)[...] = total.astype(BF)
        rs_right(step, ch).start()

    def pass_left(step, ch, add):
        total = part(acc, 5 - step, ch)[...]
        if add:
            rs_left(step - 1, ch).wait_recv()
            total = total + part(pin_r, step - 2, ch)[...].astype(F32)
        part(po, 3 + step, ch)[...] = total.astype(BF)
        rs_left(step, ch).start()

    far = [(i, CHUNKS - 1 - i) for i in range(CHUNKS // 2)]
    near = [(CHUNKS // 2 + i, CHUNKS // 2 - 1 - i) for i in range(CHUNKS // 2)]

    def pass_on(step, pairs, add):
        for r, l in pairs:
            pass_right(step, r, add)
            pass_left(step, l, add)

    pieces = hist // KEY_STEP
    for p in range(pieces):
        attend(0, 0, 0, 1, p)

    def come(t):
        k = lax.div(t, CHUNKS) + 1
        i = lax.rem(t, CHUNKS)
        return k, i, to_right(0, k, i, t), to_left(0, n_ctx - k, CHUNKS - 1 - i, t)

    last = 3 * CHUNKS

    def ring(t, _):
        k, i, from_left, from_right = come(t)
        from_left.wait_recv()
        to_right(k, k + 1, i, t + CHUNKS).start()
        from_right.wait_recv()
        to_left(n_ctx - k, n_ctx - k - 1, CHUNKS - 1 - i, t + CHUNKS).start()

        @pl.when(lax.rem(t, CHUNKS) == CHUNKS - 1)
        def _():
            attend(1, 0, n_ctx - 1, 1, k - 1)

        return 0

    lax.fori_loop(0, last - CHUNKS, ring, 0)

    arrived(sf, rf, sf_ss, sf_rs)
    q_all[4] = dot(unhot_f[...], rf[...].reshape(slot_total, width)).astype(BF)

    def attend_piece(block_a, half_a, block_b, half_b):
        def body(p, _):
            attend(block_a, half_a, block_b, half_b, p)
            return 0

        lax.fori_loop(0, pieces, body, 0)

    attend_piece(4, 0, 4, 1)
    pass_on(1, far, False)
    sg[...] = dot(hot_v[...], tab_g[...]).astype(BF).reshape(sg.shape)
    exchange(sg, rg, sg_ss, sg_rs)

    def land(t, _):
        k, i, from_left, from_right = come(t)
        from_left.wait_recv()
        from_right.wait_recv()
        return 0

    lax.fori_loop(last - CHUNKS, last - CHUNKS // 2, land, 0)
    attend_piece(3, 0, 5, 1)
    pass_on(2, near, False)
    lax.fori_loop(last - CHUNKS // 2, last, land, 0)
    attend_piece(3, 1, 5, 0)
    pass_on(2, far, True)
    attend_piece(2, 0, 6, 1)
    pass_on(3, near, True)
    attend_piece(2, 1, 6, 0)
    pass_on(3, far, True)
    attend_piece(1, 1, 7, 0)
    pass_on(4, near, True)
    pass_on(4, far, True)
    arrived(sg, rg, sg_ss, sg_rs)
    gate_v[...] = dot(unhot_v[...], rg[...].reshape(slot_total, width))

    def xg_copy(k, ch):
        return send(part(g_all, 0, ch), part(g_all, k, ch), xg_ss.at[k, ch], xg_rs.at[k, ch],
                    "head", lax.rem(h + k, n_head))

    order = [ch for pair in far for ch in pair]
    for ch in order:
        rs_right(4, ch).wait_recv()
        rs_left(4, ch).wait_recv()
        attended = part(acc, 0, ch)[...] + part(pin_l, 3, ch)[...].astype(F32) + part(pin_r, 3, ch)[...].astype(F32)
        rows = slice(ch * chunk, (ch + 1) * chunk)
        part(g_all, 0, ch)[...] = (attended * gate_v[rows]).astype(BF)
        for k in (2, 1, 3):
            xg_copy(k, ch).start()

    for k in range(1, n_head):
        wx_copy(k).wait_recv()
    for ch in order:
        total = dot(part(g_all, 0, ch)[...], wx[0])
        for k in (1, 3, 2):
            xg_copy(k, ch).wait_recv()
            total = total + dot(part(g_all, k, ch)[...], wx[k])
        out_ref[ch * chunk:(ch + 1) * chunk] = total.astype(BF)

    drained(req_out, req_in, req_ss, req_rs)
    drained(sq, rq, sq_ss, sq_rs)
    drained(sf, rf, sf_ss, sf_rs)
    ids_copy.wait_send()
    req_copy.wait_send()
    drained(sg, rg, sg_ss, sg_rs)
    for k in range(1, n_head):
        wx_copy(k).wait_send()
        for ch in range(CHUNKS):
            xg_copy(k, ch).wait_send()
    for number in range(last):
        to_right(0, 1, 0, number).wait_send()
        to_left(0, 1, 0, number).wait_send()
    for step in range(1, 5):
        for r, l in far if step == 1 else far + near:
            rs_right(step, r).wait_send()
            rs_left(step, l).wait_send()


def per_device(catalog, cand_owner, cand_row, hist_len, proj_weight, keys, values, out_weight):
    n_user, n_ctx, n_head = (lax.axis_size(a) for a in ("user", "ctx", "head"))
    cand = cand_row.shape[1]
    rows, model = catalog.shape
    hist, width = keys.shape[1:]
    slots = n_user * SLOTS
    any_space = pl.BlockSpec(memory_space=pltpu.HBM)
    vmem = pl.BlockSpec(memory_space=pltpu.VMEM)
    dma = pltpu.SemaphoreType.DMA
    piece = (n_user, SLOTS, width)
    ranked = pl.pallas_call(
        functools.partial(kernel, n_user, n_ctx, n_head),
        out_shape=jax.ShapeDtypeStruct((cand, width), BF),
        in_specs=[any_space] * 8,
        out_specs=vmem,
        scratch_shapes=[
            pltpu.VMEM((1, cand), jnp.int32),
            pltpu.VMEM((1, cand), jnp.int32),
            pltpu.SMEM((1,), jnp.int32),
            pltpu.VMEM((rows, model), BF),
            pltpu.VMEM((model, 2, width), BF),
            pltpu.VMEM((2, model, width), BF),
            pltpu.VMEM((hist, width), BF),
            pltpu.VMEM((hist, width), BF),
            pltpu.VMEM((width, model), BF),
            pltpu.VMEM((n_user, 1, 128), jnp.int32),
            pltpu.VMEM((n_user, 1, 128), jnp.int32),
            pltpu.VMEM((rows, width), BF),
            pltpu.VMEM((rows, width), BF),
            pltpu.VMEM((slots, rows), BF),
            pltpu.VMEM((cand, slots), BF),
            pltpu.VMEM(piece, BF),
            pltpu.VMEM(piece, BF),
            pltpu.VMEM(piece, BF),
            pltpu.VMEM(piece, BF),
            pltpu.VMEM((1, cand), jnp.int32),
            pltpu.VMEM((n_user, 1, 128), jnp.int32),
            pltpu.VMEM((slots, rows), BF),
            pltpu.VMEM((cand, slots), BF),
            pltpu.VMEM(piece, BF),
            pltpu.VMEM(piece, BF),
            pltpu.VMEM((n_ctx, cand, width), BF),
            pltpu.VMEM((n_ctx, cand, width), F32),
            pltpu.VMEM((8, cand, width), BF),
            pltpu.VMEM((4, cand, width), BF),
            pltpu.VMEM((4, cand, width), BF),
            pltpu.VMEM((cand, width), F32),
            pltpu.VMEM((n_head, cand, width), BF),
            pltpu.VMEM((n_head, width, width), BF),
            dma((8,)),
            dma((n_user,)), dma((n_user,)),
            dma((n_user,)), dma((n_user,)),
            dma((n_user,)), dma((n_user,)),
            dma((2,)), dma((2,)),
            dma((n_user,)), dma((n_user,)),
            dma((2, 3 * CHUNKS)), dma((2, 3 * CHUNKS)),
            dma((2, 4, CHUNKS)), dma((2, 4, CHUNKS)),
            dma((n_head,)), dma((n_head,)),
            dma((n_head, CHUNKS)), dma((n_head, CHUNKS)),
        ],
        compiler_params=pltpu.CompilerParams(
            collective_id=0, has_side_effects=True, vmem_limit_bytes=55000 * 2**10
        ),
        name="rank_items",
    )(
        catalog,
        cand_owner.reshape(1, cand),
        cand_row,
        hist_len,
        proj_weight,
        keys.reshape(hist, width),
        values.reshape(hist, width),
        out_weight,
    )
    return ranked.reshape(1, cand, width)


def solution(mesh):
    return jax.shard_map(
        per_device,
        mesh=mesh,
        in_specs=(
            P("user", None),
            P("user", "ctx", None),
            P("user", "ctx"),
            P("user"),
            P(None, None, "head"),
            P("user", "ctx", "head"),
            P("user", "ctx", "head"),
            P("head", None),
        ),
        out_specs=P("user", "ctx", "head"),
        check_vma=False,
    )
```

```python
import functools

import jax
import jax.numpy as jnp
from jax import lax
from jax.experimental import pallas as pl
from jax.experimental.pallas import tpu as pltpu
from jax.sharding import PartitionSpec as P

HEAD = 128
MESH = pl.DeviceIdType.MESH
BF = jnp.bfloat16
F32 = jnp.float32
SLOTS = 32
KEY_STEP = 768
CHUNKS = 4


def send(src, dst, ssem, rsem, axis, index):
    return pltpu.make_async_remote_copy(
        src_ref=src, dst_ref=dst, send_sem=ssem, recv_sem=rsem,
        device_id={axis: index}, device_id_type=MESH,
    )


def column(row, lanes):
    tall = jnp.broadcast_to(row, (128, row.shape[1])).T
    return jnp.concatenate([tall] * (lanes // 128), axis=1)


def silu(v):
    return v / (1.0 + jnp.exp(-v))


def dot(a, b):
    return jnp.dot(a, b, preferred_element_type=F32)


def dot_t(a, b):
    return lax.dot_general(a, b, (((1,), (1,)), ((), ())), preferred_element_type=F32)


def kernel(
    n_user, n_ctx, n_head,
    cat_hbm, owner_hbm, row_hbm, len_hbm, w_hbm, key_hbm, val_hbm, wout_hbm,
    out_ref,
    owner_ref, row_ref, len_ref, cat_v, w_pairs, w_v, key_v, val_v, wout_v,
    req_out, req_in, tab_q, tab_g, hot_v, unhot_v, sq, sg, rq, rg,
    ids_f, req_f, hot_f, unhot_f, sf, rf,
    q_all, acc, po, pin_l, pin_r, gate_v, g_all, wx,
    load_sem, req_ss, req_rs, sq_ss, sq_rs, sf_ss, sf_rs, opp_ss, opp_rs, sg_ss, sg_rs,
    ag_ss, ag_rs, rs_ss, rs_rs, wx_ss, wx_rs, xg_ss, xg_rs,
):
    u = lax.axis_index("user")
    c = lax.axis_index("ctx")
    h = lax.axis_index("head")
    right, left = lax.rem(c + 1, n_ctx), lax.rem(c + n_ctx - 1, n_ctx)
    opposite = lax.rem(c + n_ctx // 2, n_ctx)
    cand = owner_ref.shape[1]
    half = cand // 2
    chunk = cand // CHUNKS
    hist = key_v.shape[0]
    width = key_v.shape[1]
    model = cat_v.shape[1]
    slot_total = n_user * SLOTS

    barrier = pltpu.get_barrier_semaphore()

    def greet(d, _):
        pl.semaphore_signal(barrier, inc=1, device_id={"user": lax.rem(u + d, n_user)}, device_id_type=MESH)
        return 0

    lax.fori_loop(1, n_user, greet, 0)
    for other in (left, right, opposite):
        pl.semaphore_signal(barrier, inc=1, device_id={"ctx": other}, device_id_type=MESH)
    for k in range(1, n_head):
        pl.semaphore_signal(barrier, inc=1, device_id={"head": lax.rem(h + k, n_head)}, device_id_type=MESH)

    loads = [
        pltpu.make_async_copy(a, b, load_sem.at[i])
        for i, (a, b) in enumerate(
            ((cat_hbm, cat_v), (w_hbm, w_pairs), (wout_hbm, wout_v), (key_hbm, key_v), (val_hbm, val_v),
             (owner_hbm, owner_ref), (row_hbm, row_ref), (len_hbm, len_ref))
        )
    ]
    for copy in loads[5:] + loads[:5]:
        copy.start()
    loads[5].wait()
    loads[6].wait()

    slot_lane = lax.broadcasted_iota(jnp.int32, (cand, slot_total), 1).astype(F32)

    def places(ids):
        owner = ids.astype(F32)
        owner_col = column(owner, cand)
        first = lax.broadcasted_iota(jnp.int32, (cand, cand), 0)
        second = lax.broadcasted_iota(jnp.int32, (cand, cand), 1)
        before = jnp.where((owner_col == owner) & (first < second), 1.0, 0.0)
        rank = jnp.sum(before, axis=0, keepdims=True)
        place_col = column(owner * SLOTS + rank, slot_total)
        return owner_col, place_col, jnp.where(place_col == slot_lane, 1.0, 0.0).astype(BF)

    owner_col, place_col, unhot_v[...] = places(owner_ref[...])
    rank_col = place_col[:, :128] - owner_col[:, :128] * SLOTS
    shift = (lax.rem(u, 4) * SLOTS).astype(F32)
    rank_hot = jnp.where(rank_col + shift == slot_lane[:, :128], 1.0, 0.0).astype(BF)
    wanted = row_ref[...]
    shard = lax.broadcasted_iota(jnp.int32, (n_user, cand), 0)
    mine = owner_ref[...] == shard
    high = jnp.where(mine, lax.shift_right_logical(wanted, 4).astype(F32), 0.0)
    low = jnp.where(mine, (wanted & 15).astype(F32), 0.0)
    asked = dot(jnp.concatenate([high, low], axis=0).astype(BF), rank_hot)
    asked = (asked[:n_user] * 16.0 + asked[n_user:]).astype(jnp.int32)
    for s in range(n_user):
        req_out[s] = asked[s:s + 1]

    pl.semaphore_wait(barrier, n_user - 1 + 3 + n_head - 1)

    def exchange(src, dst, ssem, rsem):
        def start(d, _):
            to = lax.rem(u + d, n_user)
            send(src.at[to], dst.at[u], ssem.at[d], rsem.at[d], "user", to).start()
            return 0

        lax.fori_loop(1, n_user, start, 0)
        dst[u] = src[u]

    def arrived(src, dst, ssem, rsem):
        def wait(d, _):
            origin = lax.rem(u + n_user - d, n_user)
            send(src.at[0], dst.at[origin], ssem.at[d], rsem.at[d], "user", lax.rem(u + d, n_user)).wait_recv()
            return 0

        lax.fori_loop(1, n_user, wait, 0)

    def drained(src, dst, ssem, rsem):
        def wait(d, _):
            to = lax.rem(u + d, n_user)
            send(src.at[to], dst.at[u], ssem.at[d], rsem.at[d], "user", to).wait_send()
            return 0

        lax.fori_loop(1, n_user, wait, 0)

    ids_copy = send(owner_ref, ids_f, opp_ss.at[0], opp_rs.at[0], "ctx", opposite)
    req_copy = send(req_in, req_f, opp_ss.at[1], opp_rs.at[1], "ctx", opposite)
    exchange(req_out, req_in, req_ss, req_rs)
    ids_copy.start()

    loads[0].wait()
    loads[1].wait()
    to = lax.broadcasted_iota(jnp.int32, (256, 256), 0)
    source = jnp.where(to < 128, 2 * to, 2 * to - 255)
    split = jnp.where(source == lax.broadcasted_iota(jnp.int32, (256, 256), 1), 1.0, 0.0).astype(BF)
    pairs = w_pairs[...].reshape(2 * model, width)
    for i in range(model // 128):
        apart = dot(split, pairs[256 * i:256 * (i + 1)]).astype(BF)
        w_v[0, 128 * i:128 * (i + 1)] = apart[:128]
        w_v[1, 128 * i:128 * (i + 1)] = apart[128:]
    tab_q[...] = silu(dot(cat_v[...], w_v[0])).astype(BF)
    tab_g[...] = silu(dot(cat_v[...], w_v[1])).astype(BF)

    loads[2].wait()

    def wx_copy(k):
        to = lax.rem(h + k, n_head)
        cols = pl.ds(pl.multiple_of(to * width, width), width)
        return send(wout_v.at[:, cols], wx.at[k], wx_ss.at[k], wx_rs.at[k], "head", to)

    for k in range(1, n_head):
        wx_copy(k).start()
    wx[0] = wout_v[:, pl.ds(pl.multiple_of(h * width, width), width)]

    acc[...] = jnp.zeros_like(acc)
    arrived(req_out, req_in, req_ss, req_rs)
    req_copy.start()
    row_lane = lax.broadcasted_iota(jnp.int32, (128, cat_v.shape[0]), 1).astype(F32)

    def serve(requests, hot_ref, src, dst, ssem, rsem):
        def group(g, _):
            four = lax.rem(lax.div(u, 4) + g, n_user // 4) * 4
            ids = requests[four] + requests[four + 1] + requests[four + 2] + requests[four + 3]
            hot = jnp.where(column(ids.astype(F32), cat_v.shape[0]) == row_lane, 1.0, 0.0).astype(BF)
            hot_ref[pl.ds(pl.multiple_of(four * SLOTS, 128), 128)] = hot
            src[pl.ds(four, 4)] = dot(hot, tab_q[...]).astype(BF).reshape(4, SLOTS, width)
            for i in range(4):
                d = lax.rem(four + i - u + n_user, n_user)

                @pl.when(d > 0)
                def _():
                    send(src.at[four + i], dst.at[u], ssem.at[d], rsem.at[d], "user", four + i).start()

            return 0

        lax.fori_loop(1, n_user // 4 + 1, group, 0)
        dst[u] = src[u]

    serve(req_in, hot_v, sq, rq, sq_ss, sq_rs)

    req_copy.wait_recv()
    serve(req_f, hot_f, sf, rf, sf_ss, sf_rs)

    sg[...] = dot(hot_v[...], tab_g[...]).astype(BF).reshape(sg.shape)
    arrived(sq, rq, sq_ss, sq_rs)
    q_all[0] = dot(unhot_v[...], rq[...].reshape(slot_total, width)).astype(BF)

    def part(ref, block, ch):
        return ref.at[block, pl.ds(pl.multiple_of(ch * chunk, chunk), chunk)]

    def half_of(ref, block, j):
        return ref.at[block, pl.ds(pl.multiple_of(j * half, half), half)]

    def to_right(src_block, dst_block, ch, number):
        return send(part(q_all, src_block, ch), part(q_all, dst_block, ch),
                    ag_ss.at[0, number], ag_rs.at[0, number], "ctx", right)

    def to_left(src_block, dst_block, ch, number):
        return send(part(q_all, src_block, ch), part(q_all, dst_block, ch),
                    ag_ss.at[1, number], ag_rs.at[1, number], "ctx", left)

    for i in range(CHUNKS):
        to_right(0, 1, i, i).start()
        to_left(0, n_ctx - 1, CHUNKS - 1 - i, i).start()

    ids_copy.wait_recv()
    unhot_f[...] = places(ids_f[...])[2]

    loads[3].wait()
    loads[4].wait()
    loads[7].wait()
    length = len_ref[0]
    place = lax.broadcasted_iota(jnp.int32, (hist, width), 0) + c * hist
    val_v[...] = jnp.where(place < length, val_v[...].astype(F32), 0.0).astype(BF)
    scale = HEAD ** -0.5
    arg_scale = 0.5 * scale
    out_scale = (0.5 * scale) / jnp.full((1, KEY_STEP), length, jnp.int32).astype(F32)

    def attend(block_a, half_a, block_b, half_b, piece):
        queries = jnp.concatenate([half_of(q_all, block_a, half_a)[...], half_of(q_all, block_b, half_b)[...]], axis=0)
        rows = pl.ds(pl.multiple_of(piece * KEY_STEP, KEY_STEP), KEY_STEP)
        terms = []
        for n in range(width // HEAD):
            cols = pl.ds(n * HEAD, HEAD)
            scores = dot_t(queries[:, n * HEAD:(n + 1) * HEAD], key_v[rows, cols])
            scaled = scores * out_scale
            weights = (scaled + scaled * jnp.tanh(scores * arg_scale)).astype(BF)
            terms.append(dot(weights, val_v[rows, cols]))
        mixed = jnp.concatenate(terms, axis=1)
        half_of(acc, block_a, half_a)[...] += mixed[:half]
        half_of(acc, block_b, half_b)[...] += mixed[half:]

    def rs_right(step, ch):
        return send(part(po, step - 1, ch), part(pin_l, step - 1, ch),
                    rs_ss.at[0, step - 1, ch], rs_rs.at[0, step - 1, ch], "ctx", right)

    def rs_left(step, ch):
        return send(part(po, 3 + step, ch), part(pin_r, step - 1, ch),
                    rs_ss.at[1, step - 1, ch], rs_rs.at[1, step - 1, ch], "ctx", left)

    def pass_right(step, ch, add):
        total = part(acc, 3 + step, ch)[...]
        if add:
            rs_right(step - 1, ch).wait_recv()
            total = total + part(pin_l, step - 2, ch)[...].astype(F32)
        part(po, step - 1, ch)[...] = total.astype(BF)
        rs_right(step, ch).start()

    def pass_left(step, ch, add):
        total = part(acc, 5 - step, ch)[...]
        if add:
            rs_left(step - 1, ch).wait_recv()
            total = total + part(pin_r, step - 2, ch)[...].astype(F32)
        part(po, 3 + step, ch)[...] = total.astype(BF)
        rs_left(step, ch).start()

    far = [(i, CHUNKS - 1 - i) for i in range(CHUNKS // 2)]
    near = [(CHUNKS // 2 + i, CHUNKS // 2 - 1 - i) for i in range(CHUNKS // 2)]

    def pass_on(step, pairs, add):
        for r, l in pairs:
            pass_right(step, r, add)
            pass_left(step, l, add)

    pieces = hist // KEY_STEP
    for p in range(pieces):
        attend(0, 0, 0, 1, p)

    def come(t):
        k = lax.div(t, CHUNKS) + 1
        i = lax.rem(t, CHUNKS)
        return k, i, to_right(0, k, i, t), to_left(0, n_ctx - k, CHUNKS - 1 - i, t)

    last = 3 * CHUNKS

    def ring(t, _):
        k, i, from_left, from_right = come(t)
        from_left.wait_recv()
        to_right(k, k + 1, i, t + CHUNKS).start()
        from_right.wait_recv()
        to_left(n_ctx - k, n_ctx - k - 1, CHUNKS - 1 - i, t + CHUNKS).start()

        @pl.when(lax.rem(t, CHUNKS) == CHUNKS - 1)
        def _():
            attend(1, 0, n_ctx - 1, 1, k - 1)

        return 0

    lax.fori_loop(0, last - CHUNKS, ring, 0)

    arrived(sf, rf, sf_ss, sf_rs)
    q_all[4] = dot(unhot_f[...], rf[...].reshape(slot_total, width)).astype(BF)

    def attend_piece(block_a, half_a, block_b, half_b):
        def body(p, _):
            attend(block_a, half_a, block_b, half_b, p)
            return 0

        lax.fori_loop(0, pieces, body, 0)

    attend_piece(4, 0, 4, 1)
    pass_on(1, far, False)
    exchange(sg, rg, sg_ss, sg_rs)

    def land(t, _):
        k, i, from_left, from_right = come(t)
        from_left.wait_recv()
        from_right.wait_recv()
        return 0

    lax.fori_loop(last - CHUNKS, last - CHUNKS // 2, land, 0)
    attend_piece(3, 0, 5, 1)
    pass_on(2, near, False)
    lax.fori_loop(last - CHUNKS // 2, last, land, 0)
    attend_piece(3, 1, 5, 0)
    pass_on(2, far, True)
    attend_piece(2, 0, 6, 1)
    pass_on(3, near, True)
    attend_piece(2, 1, 6, 0)
    pass_on(3, far, True)
    attend_piece(1, 1, 7, 0)
    pass_on(4, near, True)
    pass_on(4, far, True)
    arrived(sg, rg, sg_ss, sg_rs)
    gate_v[...] = dot(unhot_v[...], rg[...].reshape(slot_total, width))

    def xg_copy(k, ch):
        return send(part(g_all, 0, ch), part(g_all, k, ch), xg_ss.at[k, ch], xg_rs.at[k, ch],
                    "head", lax.rem(h + k, n_head))

    order = [ch for pair in far for ch in pair]
    for ch in order:
        rs_right(4, ch).wait_recv()
        rs_left(4, ch).wait_recv()
        attended = part(acc, 0, ch)[...] + part(pin_l, 3, ch)[...].astype(F32) + part(pin_r, 3, ch)[...].astype(F32)
        rows = slice(ch * chunk, (ch + 1) * chunk)
        part(g_all, 0, ch)[...] = (attended * gate_v[rows]).astype(BF)
        for k in (2, 1, 3):
            xg_copy(k, ch).start()

    for k in range(1, n_head):
        wx_copy(k).wait_recv()
    for ch in order:
        total = dot(part(g_all, 0, ch)[...], wx[0])
        for k in (1, 3, 2):
            xg_copy(k, ch).wait_recv()
            total = total + dot(part(g_all, k, ch)[...], wx[k])
        out_ref[ch * chunk:(ch + 1) * chunk] = total.astype(BF)

    drained(req_out, req_in, req_ss, req_rs)
    drained(sq, rq, sq_ss, sq_rs)
    drained(sf, rf, sf_ss, sf_rs)
    ids_copy.wait_send()
    req_copy.wait_send()
    drained(sg, rg, sg_ss, sg_rs)
    for k in range(1, n_head):
        wx_copy(k).wait_send()
        for ch in range(CHUNKS):
            xg_copy(k, ch).wait_send()
    for number in range(last):
        to_right(0, 1, 0, number).wait_send()
        to_left(0, 1, 0, number).wait_send()
    for step in range(1, 5):
        for r, l in far if step == 1 else far + near:
            rs_right(step, r).wait_send()
            rs_left(step, l).wait_send()


def per_device(catalog, cand_owner, cand_row, hist_len, proj_weight, keys, values, out_weight):
    n_user, n_ctx, n_head = (lax.axis_size(a) for a in ("user", "ctx", "head"))
    cand = cand_row.shape[1]
    rows, model = catalog.shape
    hist, width = keys.shape[1:]
    slots = n_user * SLOTS
    any_space = pl.BlockSpec(memory_space=pltpu.HBM)
    vmem = pl.BlockSpec(memory_space=pltpu.VMEM)
    dma = pltpu.SemaphoreType.DMA
    piece = (n_user, SLOTS, width)
    ranked = pl.pallas_call(
        functools.partial(kernel, n_user, n_ctx, n_head),
        out_shape=jax.ShapeDtypeStruct((cand, width), BF),
        in_specs=[any_space] * 8,
        out_specs=vmem,
        scratch_shapes=[
            pltpu.VMEM((1, cand), jnp.int32),
            pltpu.VMEM((1, cand), jnp.int32),
            pltpu.SMEM((1,), jnp.int32),
            pltpu.VMEM((rows, model), BF),
            pltpu.VMEM((model, 2, width), BF),
            pltpu.VMEM((2, model, width), BF),
            pltpu.VMEM((hist, width), BF),
            pltpu.VMEM((hist, width), BF),
            pltpu.VMEM((width, model), BF),
            pltpu.VMEM((n_user, 1, 128), jnp.int32),
            pltpu.VMEM((n_user, 1, 128), jnp.int32),
            pltpu.VMEM((rows, width), BF),
            pltpu.VMEM((rows, width), BF),
            pltpu.VMEM((slots, rows), BF),
            pltpu.VMEM((cand, slots), BF),
            pltpu.VMEM(piece, BF),
            pltpu.VMEM(piece, BF),
            pltpu.VMEM(piece, BF),
            pltpu.VMEM(piece, BF),
            pltpu.VMEM((1, cand), jnp.int32),
            pltpu.VMEM((n_user, 1, 128), jnp.int32),
            pltpu.VMEM((slots, rows), BF),
            pltpu.VMEM((cand, slots), BF),
            pltpu.VMEM(piece, BF),
            pltpu.VMEM(piece, BF),
            pltpu.VMEM((n_ctx, cand, width), BF),
            pltpu.VMEM((n_ctx, cand, width), F32),
            pltpu.VMEM((8, cand, width), BF),
            pltpu.VMEM((4, cand, width), BF),
            pltpu.VMEM((4, cand, width), BF),
            pltpu.VMEM((cand, width), F32),
            pltpu.VMEM((n_head, cand, width), BF),
            pltpu.VMEM((n_head, width, width), BF),
            dma((8,)),
            dma((n_user,)), dma((n_user,)),
            dma((n_user,)), dma((n_user,)),
            dma((n_user,)), dma((n_user,)),
            dma((2,)), dma((2,)),
            dma((n_user,)), dma((n_user,)),
            dma((2, 3 * CHUNKS)), dma((2, 3 * CHUNKS)),
            dma((2, 4, CHUNKS)), dma((2, 4, CHUNKS)),
            dma((n_head,)), dma((n_head,)),
            dma((n_head, CHUNKS)), dma((n_head, CHUNKS)),
        ],
        compiler_params=pltpu.CompilerParams(
            collective_id=0, has_side_effects=True, vmem_limit_bytes=55000 * 2**10
        ),
        name="rank_items",
    )(
        catalog,
        cand_owner.reshape(1, cand),
        cand_row,
        hist_len,
        proj_weight,
        keys.reshape(hist, width),
        values.reshape(hist, width),
        out_weight,
    )
    return ranked.reshape(1, cand, width)


def solution(mesh):
    return jax.shard_map(
        per_device,
        mesh=mesh,
        in_specs=(
            P("user", None),
            P("user", "ctx", None),
            P("user", "ctx"),
            P("user"),
            P(None, None, "head"),
            P("user", "ctx", "head"),
            P("user", "ctx", "head"),
            P("head", None),
        ),
        out_specs=P("user", "ctx", "head"),
        check_vma=False,
    )
```
